256 devices in a mesh: section: 2 (over y_hi), dp: 8 (over x, core), tensor: 16 (over y_lo, z).
Axes of the slice: x: 4, y: 4 (y_hi: 2, y_lo: 2; y = y_hi * 2 + y_lo), z: 8, core: 2. Of those that a mesh axis runs over, the one named last changes fastest.
Arguments:
- activations: bfloat16 [2, 8, 256, 3584], P(None, 'dp', 'tensor'), may hold values from -24 to 24
- norm_gain: bfloat16 [2, 3584], P('section'), may hold values from 0.099609375 to 1.8984375
- query_matrix: bfloat16 [2, 3584, 4096], P('section', None, 'tensor'), may hold values from -0.09375 to 0.09375
- key_weight: bfloat16 [2, 3584, 4096], P('section', None, 'tensor'), may hold values from -0.09375 to 0.09375
- value_weight: bfloat16 [2, 3584, 8192], P('section', None, 'tensor'), may hold values from -0.09375 to 0.09375
- decay_down: bfloat16 [2, 3584, 16], P('section'), may hold values from -0.09375 to 0.09375
- decay_up: bfloat16 [2, 16, 4096], P('section', None, 'tensor'), may hold values from -1.5 to 1.5
- decay_bias: float32 [2, 4096], P('section', 'tensor'), may hold values from -3 to 5
- head_gain: bfloat16 [2, 8192], P('section', 'tensor'), may hold values from 0.099609375 to 1.8984375
- output_matrix: bfloat16 [2, 8192, 3584], P('section', 'tensor'), may hold values from -0.0625 to 0.0625
Outputs:
- finals: bfloat16 [2, 8, 256, 3584], P('section', 'dp', 'tensor')
The draws below stay inside these ranges and needn't reach their ends.
All inputs are finite; a program needn't handle non-finite values.
Results may differ from the reference program's by a relative error of at most 0.029.
Values may be sent and summed in bfloat16 or wider, within the bound.
No kernel may reach another device: no remote copies, remote signals or barrier semaphores. Data moves between devices by JAX's collectives and lax.ppermute only.
A program may use at most 64 MiB of HBM per device.

```python
import math
import jax
import jax.numpy as jnp
from jax import lax

D = 3584
KEY = 64
VAL = 128
HEAD_DEV = 4
RANK = 16
LEN = 256
HEADS = 64
SEQS = 8
MICRO = 2
N_SECTION = 2
N_TENSOR = 16


def draw_activations(key, part):
    key = jax.random.fold_in(key, 7)
    base_key, row_key, column_key = jax.random.split(key, 3)
    full_shape = (MICRO, SEQS, LEN, D)
    row_scale = jnp.exp(jax.random.uniform(row_key, (MICRO, SEQS, LEN, 1), jnp.float32, math.log(0.3), math.log(3.0)))
    column_scale = jnp.exp(jax.random.uniform(column_key, (D,), jnp.float32, math.log(0.5), math.log(2.0)))
    value_rows_start = jnp.clip(jax.random.normal(base_key, full_shape, jnp.float32), -4.0, 4.0)
    return (value_rows_start * row_scale * column_scale).astype(jnp.bfloat16)


def shard_levels(rng, extent, cuts, least, largest):
    def one(axis_at, parts):
        heights = jax.random.uniform(jax.random.fold_in(jax.random.fold_in(rng, 6), axis_at), (parts,), jnp.float32, least / len(cuts), largest / len(cuts))
        return jnp.repeat(jnp.exp(heights), extent[axis_at] // parts).reshape((-1,) + (1,) * (len(extent) - axis_at - 1))

    factor_of = one(*cuts[0])
    for cut in cuts[1:]:
        factor_of = factor_of * one(*cut)
    return factor_of


def scatter_about(rng, dims, spread, limit, cuts=(), kind=jnp.bfloat16):
    level = shard_levels(rng, dims, cuts, -0.22, 0.18) if cuts else 1.0
    result = jax.random.normal(rng, dims, jnp.float32) * spread * level
    return jnp.minimum(jnp.maximum(result, -limit), limit).astype(kind)


def setup_inputs(seed: int = 0) -> dict:
    arg_keys = jax.random.split(jax.random.key(seed), 11)
    return {
        "activations": draw_activations(jax.random.fold_in(arg_keys[10], 71), 0),
        "norm_gain": jnp.clip(1.0 + 0.18 * jax.random.normal(arg_keys[1], (N_SECTION, D), jnp.float32), 0.099609375, 1.8984375).astype(jnp.bfloat16),
        "query_matrix": scatter_about(arg_keys[2], (N_SECTION, D, HEADS * KEY), D ** -0.5, 0.09375, ((0, 2), (2, 16))),
        "key_weight": scatter_about(arg_keys[3], (N_SECTION, D, HEADS * KEY), D ** -0.5, 0.09375, ((0, 2), (2, 16))),
        "value_weight": scatter_about(arg_keys[4], (N_SECTION, D, HEADS * VAL), D ** -0.5, 0.09375, ((0, 2), (2, 16))),
        "decay_down": scatter_about(arg_keys[5], (N_SECTION, D, RANK), D ** -0.5, 0.09375, ((0, 2),)),
        "decay_up": scatter_about(arg_keys[6], (N_SECTION, RANK, HEADS * KEY), RANK ** -0.5, 1.5, ((0, 2), (2, 16))),
        "decay_bias": jnp.clip(-3.0 + 8.0 * jax.random.uniform(arg_keys[7], (N_SECTION, HEADS * KEY), jnp.float32) ** shard_levels(arg_keys[7], (N_SECTION, HEADS * KEY), ((0, 2), (1, 16)), -0.2, 0.2), -3.0, 5.0),
        "head_gain": jnp.clip(1.0 + 0.18 * jax.random.normal(arg_keys[8], (N_SECTION, HEADS * VAL), jnp.float32), 0.099609375, 1.8984375).astype(jnp.bfloat16),
        "output_matrix": scatter_about(arg_keys[9], (N_SECTION, HEADS * VAL, D), (HEADS * VAL) ** -0.5, 0.0625, ((0, 2), (1, 16))),
    }


HIGH = lax.Precision.HIGHEST

def normalize(values, gain):
    return values * lax.rsqrt(lax.optimization_barrier(jnp.mean(values * values, axis=-1, keepdims=True)) + 1e-05) * gain

def head_normalize(values, gain):
    return values * lax.rsqrt(jnp.maximum(lax.optimization_barrier(jnp.mean(values * values, axis=-1, keepdims=True)), 1.0)) * gain

def recurrence(query, keys, values, decay_logarithm):

    def advance(state, inputs):
        q_now, k_now, v_now, lg_now = inputs
        state = jnp.exp(lg_now)[..., None] * state + k_now[..., :, None] * v_now[..., None, :]
        return (state, jnp.einsum('shk,shkv->shv', q_now, state, precision=HIGH))
    start_state = jnp.zeros((query.shape[0], query.shape[2], KEY, VAL), jnp.float32)
    inputs = tuple((jnp.moveaxis(item, 1, 0) for item in (query, keys, values, decay_logarithm)))
    _, outputs = lax.scan(advance, start_state, inputs)
    return jnp.moveaxis(outputs, 0, 1)

def layer(hidden, section_slot, norm_gain, query_matrix, key_weight, value_weight, decay_down, decay_up, decay_bias, head_gain, output_matrix):
    count = SEQS * LEN
    stream = hidden.reshape(count, D).astype(jnp.float32)
    normed = normalize(stream, norm_gain[section_slot].astype(jnp.float32)).astype(jnp.bfloat16)
    query = jnp.dot(normed, query_matrix[section_slot], preferred_element_type=jnp.float32).astype(jnp.bfloat16)
    keys = jnp.dot(normed, key_weight[section_slot], preferred_element_type=jnp.float32).astype(jnp.bfloat16)
    values = jnp.dot(normed, value_weight[section_slot], preferred_element_type=jnp.float32).astype(jnp.bfloat16)
    low_rank = jnp.dot(normed, decay_down[section_slot], preferred_element_type=jnp.float32).astype(jnp.bfloat16)
    rate_logit = jnp.dot(low_rank, decay_up[section_slot], preferred_element_type=jnp.float32) + decay_bias[section_slot].astype(jnp.float32)
    decay_logarithm = jax.nn.log_sigmoid(rate_logit) / 16.0
    key_shape = (SEQS, LEN, HEADS, KEY)
    mixed = recurrence(query.astype(jnp.float32).reshape(key_shape) * KEY ** (-0.5), keys.astype(jnp.float32).reshape(key_shape), values.astype(jnp.float32).reshape(SEQS, LEN, HEADS, VAL), decay_logarithm.reshape(key_shape))
    head_scale = head_gain[section_slot].astype(jnp.float32).reshape(HEADS, VAL)
    gated = head_normalize(mixed, head_scale).astype(jnp.bfloat16).reshape(count, HEADS * VAL)
    group_width = HEAD_DEV * VAL

    def add_group(total, group_index):
        block = lax.dynamic_slice_in_dim(gated, group_index * group_width, group_width, 1)
        rows_of_weight = lax.dynamic_slice_in_dim(output_matrix[section_slot], group_index * group_width, group_width, 0)
        term = jnp.dot(block, rows_of_weight, preferred_element_type=jnp.float32)
        term = lax.optimization_barrier(term.astype(jnp.bfloat16)).astype(jnp.float32)
        return (total + term, None)
    projected, _ = lax.scan(add_group, jnp.zeros((count, D), jnp.float32), jnp.arange(N_TENSOR, dtype=jnp.int32))
    return (stream + projected).astype(jnp.bfloat16).reshape(SEQS, LEN, D)

def reference(activations, norm_gain, query_matrix, key_weight, value_weight, decay_down, decay_up, decay_bias, head_gain, output_matrix):
    weights = (norm_gain, query_matrix, key_weight, value_weight, decay_down, decay_up, decay_bias, head_gain, output_matrix)
    section_results = []
    for batch_index in range(MICRO):
        first = layer(activations[batch_index], 0, *weights)
        section_results.append(layer(first, 1, *weights))
    return jnp.stack(section_results)
```

```python
import functools

import jax
import jax.numpy as jnp
from jax import lax
from jax.experimental import pallas as pl
from jax.experimental.pallas import tpu as pltpu
from jax.sharding import PartitionSpec as P

Z = 8
KEY = 64
VAL = 128
LEN = 256
RANK = 16
PACK = 40
OFFSETS = (0, 1, 2, 3, 5, 6, 7)
ALL = ("section", "dp", "tensor")


def zp(value):
    return lax.ppermute(value, "tensor", [(y * Z + z, y * Z + (z + 1) % Z) for y in range(2) for z in range(Z)])


def zm(value):
    return lax.ppermute(value, "tensor", [(y * Z + z, y * Z + (z + Z - 1) % Z) for y in range(2) for z in range(Z)])


def yswap(value):
    return lax.ppermute(value, "tensor", [(t, t ^ Z) for t in range(2 * Z)])


def to_second(value):
    n = 2 * Z
    return lax.ppermute(value, ("section", "tensor"), [(t, n + (t ^ Z)) for t in range(n)])


def to_first(value, cores):
    n, dp = 2 * Z, lax.axis_size("dp")
    pairs = [(dp * n + d * n + t, d * n + (t ^ Z)) for d in range(dp) if d % 2 in cores for t in range(n)]
    return lax.ppermute(value, ALL, pairs)


def to_sibling(value, core):
    dp = lax.axis_size("dp")
    return lax.ppermute(value, ("section", "dp"), [(d, d ^ 1) for d in range(dp) if d % 2 == core])


def normalize(values, gain):
    return values * lax.rsqrt(jnp.mean(values * values, axis=-1, keepdims=True) + 1e-05) * gain


def gather_ring(block):
    half = block.shape[0] // 2
    p1, m1 = zp(block), zm(block)
    p2, m2 = zp(p1), zm(m1)
    p3, m3 = zp(p2), zm(m2)
    p4, m4 = zp(p3[:half]), zm(m3[half:])
    return {0: block, 7: p1, 6: p2, 5: p3, 1: m1, 2: m2, 3: m3}, p4, m4


def add(a, b):
    return (a.astype(jnp.float32) + b.astype(jnp.float32)).astype(jnp.bfloat16)


def scatter_ring(terms, four_a, four_b):
    half = four_a.shape[0]
    p, m = zp(four_a), zm(four_b)
    up = jnp.concatenate([add(terms[3][:half], p), terms[3][half:]], 0)
    down = jnp.concatenate([terms[5][:half], add(terms[5][half:], m)], 0)
    p, m = zp(up), zm(down)
    p, m = zp(add(terms[2], p)), zm(add(terms[6], m))
    p, m = zp(add(terms[1], p)), zm(add(terms[7], m))
    return terms[0].astype(jnp.float32) + p.astype(jnp.float32) + m.astype(jnp.float32)


def nt(a, b):
    return lax.dot_general(a, b, (((1,), (1,)), ((), ())), preferred_element_type=jnp.float32)


def mix(q, k, v, low, up, bias, gain):
    width = q.shape[1]
    heads = width // KEY
    half = LEN // 2
    logits = jnp.dot(low, up, preferred_element_type=jnp.float32) + bias
    log_sig = jnp.minimum(logits, 0.0) - jnp.log1p(jnp.exp(-jnp.abs(logits)))
    decay = jnp.exp(log_sig * (1.0 / 16.0))
    q = q.astype(jnp.float32) * KEY ** -0.5
    k = k.astype(jnp.float32)
    row = lax.broadcasted_iota(jnp.int32, (LEN, width), 0)
    lane_head = lax.broadcasted_iota(jnp.int32, (1, width), 1) // KEY
    head_masks = [jnp.where(lane_head == h, 1.0, 0.0).astype(jnp.bfloat16) for h in range(heads)]
    i = lax.broadcasted_iota(jnp.int32, (heads, half, half), 1)
    j = lax.broadcasted_iota(jnp.int32, (heads, half, half), 2)

    def scores(qb, kb, rows, columns):
        lhs = jnp.concatenate([qb[rows] * m for m in head_masks], axis=0)
        return nt(lhs, kb[columns]).reshape(heads, half, half)

    first, second = slice(0, half), slice(half, LEN)
    qb, kb = q.astype(jnp.bfloat16), k.astype(jnp.bfloat16)
    att = [jnp.where(i == j, scores(qb, kb, s, s), 0.0) for s in (first, second)]
    prefix, suffix, total = decay, jnp.ones_like(decay), decay
    b = 1
    while b < half:
        qb, kb = (q * prefix).astype(jnp.bfloat16), (k * suffix).astype(jnp.bfloat16)
        mask = ((i // (2 * b)) == (j // (2 * b))) & ((i & b) != 0) & ((j & b) == 0)
        att = [jnp.where(mask, scores(qb, kb, s, s), a) for s, a in zip((first, second), att)]
        upper = (row & b) != 0
        other = jnp.where(upper, pltpu.roll(total, b, 0), pltpu.roll(total, LEN - b, 0))
        prefix = jnp.where(upper, prefix * other, prefix)
        suffix = jnp.where(upper, suffix, suffix * other)
        total = total * other
        b *= 2
    qb, kb = (q * prefix).astype(jnp.bfloat16), (k * suffix).astype(jnp.bfloat16)
    across = scores(qb, kb, second, first)
    outs = []
    for h in range(heads):
        vh = v[:, h * VAL:(h + 1) * VAL]
        top = jnp.dot(att[0][h].astype(jnp.bfloat16), vh[first], preferred_element_type=jnp.float32)
        low_part = jnp.concatenate([across[h], att[1][h]], axis=1).astype(jnp.bfloat16)
        bottom = jnp.dot(low_part, vh, preferred_element_type=jnp.float32)
        mixed = jnp.concatenate([top, bottom], axis=0)
        scale = lax.rsqrt(jnp.maximum(jnp.mean(mixed * mixed, axis=-1, keepdims=True), 1.0))
        outs.append((mixed * scale * gain[:, h * VAL:(h + 1) * VAL]).astype(jnp.bfloat16))
    return jnp.concatenate(outs, axis=1)


def layer_kernel(groups, n_sources, scalars, *refs):
    at = 0

    def take(count):
        nonlocal at
        out = refs[at:at + count]
        at += count
        return out

    blocks = take(9)
    pack, = take(1)
    sources = [take(n_sources) for _ in range(4)]
    outs = take(9)
    x, w, wo, terms, y, gated, in_sem, w_sem, out_sem = take(9)
    half = groups // 2
    z = scalars[0]
    depth = x.shape[2]

    def rows(offset):
        return pl.ds(pl.multiple_of(lax.rem(z + offset, Z) * 16, 16), 16)

    q_src, k_src, v_src, o_src = sources
    wide = w.shape[2]
    targets = [
        (q_src, slice(None), w.at[0]),
        (k_src, slice(None), w.at[1]),
        (v_src, pl.ds(0, wide), w.at[2]),
        (v_src, pl.ds(wide, wide), w.at[3]),
        (o_src, slice(None), wo),
    ]
    picks = [0, 1, 0, 0, 1]

    def weight_copy(index, which):
        src, columns, dst = targets[index]
        return pltpu.make_async_copy(src[which].at[:, columns], dst, w_sem.at[index])

    def start_weight(index):
        if n_sources == 1:
            weight_copy(index, 0).start()
            return
        choice = scalars[1 + picks[index]]
        for which in range(n_sources):
            @pl.when(choice == which)
            def _():
                weight_copy(index, which).start()

    ins = []
    for n, offset in enumerate(OFFSETS):
        ins.append(pltpu.make_async_copy(blocks[n], x.at[:, rows(offset), :], in_sem.at[n]))
    ins.append(pltpu.make_async_copy(blocks[7], x.at[pl.ds(0, half), rows(4), :], in_sem.at[7]))
    ins.append(pltpu.make_async_copy(blocks[8], x.at[pl.ds(half, half), rows(4), :], in_sem.at[8]))
    for c in ins:
        c.start()
    for index in range(5):
        start_weight(index)
    for c in ins:
        c.wait()

    xs = x.reshape(groups * 128, depth)
    down = pack[0:RANK, :].astype(jnp.bfloat16)
    low = nt(xs[...], down).astype(jnp.bfloat16)
    for index in range(4):
        weight_copy(index, 0).wait()
        y[index] = jnp.dot(xs[...], w[index], preferred_element_type=jnp.float32).astype(jnp.bfloat16)
    hg = pack[17:18, 0:2 * wide]
    bias = pack[18:19, 0:wide]
    up = pack[24:24 + RANK, 0:wide].astype(jnp.bfloat16)
    for n in range(groups // 2):
        s = slice(n * LEN, (n + 1) * LEN)
        v = jnp.concatenate([y[2, s, :], y[3, s, :]], axis=1)
        gated[s, :] = mix(y[0, s, :], y[1, s, :], v, low[s], up, bias, hg)
    weight_copy(4, 0).wait()
    ts = terms.reshape(groups * 128, depth)
    step = 512
    for c in range(depth // step):
        cols = slice(c * step, (c + 1) * step)
        ts[:, cols] = jnp.dot(gated[...], wo[:, cols], preferred_element_type=jnp.float32).astype(jnp.bfloat16)
    done = []
    for n, offset in enumerate(OFFSETS):
        done.append(pltpu.make_async_copy(terms.at[:, rows(offset), :], outs[n], out_sem.at[n]))
    done.append(pltpu.make_async_copy(terms.at[pl.ds(0, half), rows(4), :], outs[7], out_sem.at[7]))
    done.append(pltpu.make_async_copy(terms.at[pl.ds(half, half), rows(4), :], outs[8], out_sem.at[8]))
    for c in done:
        c.start()
    for c in done:
        c.wait()


def layer_call(scalars, gathered, pack, sources):
    by_offset, p4, m4 = gathered
    groups, _, depth = by_offset[0].shape
    n_sources = len(sources[0])
    count = groups * 128
    bf = jnp.bfloat16
    full = jax.ShapeDtypeStruct((groups, 16, depth), bf)
    part = jax.ShapeDtypeStruct((groups // 2, 16, depth), bf)
    anywhere = pl.BlockSpec(memory_space=pl.ANY)
    wide = sources[0][0].shape[1]
    operands = [by_offset[o] for o in OFFSETS] + [p4, m4, pack] + [a for s in sources for a in s]
    specs = [anywhere] * 9 + [pl.BlockSpec(memory_space=pltpu.VMEM)] + [anywhere] * (4 * n_sources)
    outs = pl.pallas_call(
        functools.partial(layer_kernel, groups, n_sources),
        out_shape=[full] * 7 + [part] * 2,
        in_specs=[pl.BlockSpec(memory_space=pltpu.SMEM)] + specs,
        out_specs=[anywhere] * 9,
        scratch_shapes=[
            pltpu.VMEM((groups, 128, depth), bf),
            pltpu.VMEM((4, depth, wide), bf),
            pltpu.VMEM((2 * wide, depth), bf),
            pltpu.VMEM((groups, 128, depth), bf),
            pltpu.VMEM((4, count, wide), bf),
            pltpu.VMEM((count, 2 * wide), bf),
            pltpu.SemaphoreType.DMA((9,)),
            pltpu.SemaphoreType.DMA((5,)),
            pltpu.SemaphoreType.DMA((9,)),
        ],
        compiler_params=pltpu.CompilerParams(vmem_limit_bytes=44 * 1024 * 1024),
        cost_estimate=pl.CostEstimate(
            flops=2 * count * depth * 6 * wide, bytes_accessed=12 * depth * wide + 4 * count * depth,
            transcendentals=count * wide * 3,
        ),
    )(scalars, *operands)
    return dict(zip(OFFSETS, outs[:7])), outs[7], outs[8]


def make_pack(norm_gain, decay_down, decay_up, decay_bias, head_gain):
    depth = norm_gain.shape[0]

    def wide(rows):
        rows = rows.astype(jnp.float32)
        return jnp.pad(rows, ((0, 0), (0, depth - rows.shape[1])))

    return jnp.concatenate([
        decay_down.T.astype(jnp.float32),
        norm_gain[None].astype(jnp.float32),
        wide(head_gain[None]),
        wide(decay_bias[None]),
        jnp.zeros((24 - RANK - 3, depth), jnp.float32),
        wide(decay_up),
    ], axis=0)


def per_device(activations, norm_gain, query_matrix, key_weight, value_weight, decay_down, decay_up,
               decay_bias, head_gain, output_matrix):
    section = lax.axis_index("section")
    core = lax.axis_index("dp") % 2
    tensor = lax.axis_index("tensor")
    y, z = tensor // Z, tensor % Z
    q, k, v, o = query_matrix[0], key_weight[0], value_weight[0], output_matrix[0]
    pack = make_pack(norm_gain[0], decay_down[0], decay_up[0], decay_bias[0], head_gain[0])

    pack_x = to_first(pack, (0, 1))
    v_x, k_x = to_first(v, (0,)), to_first(k, (1,))
    o_x, q_x = to_first(o, (1,)), to_first(q, (0,))
    v_d, k_d = to_sibling(v_x, 0), to_sibling(k_x, 1)
    o_d, q_d = to_sibling(o_x, 1), to_sibling(q_x, 0)

    mine = activations[:, 0]
    other = yswap(mine)
    pair = jnp.stack([jnp.where(y == 0, mine, other), jnp.where(y == 0, other, mine)], axis=1)
    normed = normalize(pair.astype(jnp.float32), norm_gain[0].astype(jnp.float32)).astype(jnp.bfloat16)
    gathered = gather_ring(normed.reshape(4, 16, -1))
    zero = jnp.zeros((), jnp.int32)
    scalars = jnp.stack([z, zero, zero]).astype(jnp.int32)
    terms = layer_call(scalars, gathered, pack, [(q,), (k,), (v,), (o,)])
    summed = scatter_ring(*terms).astype(jnp.bfloat16).reshape(2, 2, 16, -1)

    crossed = to_second(summed[1])
    own = jnp.where(section == 0, summed[0], crossed)
    partner = yswap(own)
    stream = jnp.where(section == 0, pair[0], pair[1]).astype(jnp.float32)
    stream = (stream + (own.astype(jnp.float32) + partner.astype(jnp.float32))).astype(jnp.bfloat16)
    pack_second = jnp.where(section == 0, pack_x, pack)
    normed = normalize(stream.astype(jnp.float32), pack_second[RANK]).astype(jnp.bfloat16)
    gathered = gather_ring(normed)
    pick_qv = jnp.where(section == 1, 0, jnp.where(core == 0, 1, 2))
    pick_ko = jnp.where(section == 1, 0, jnp.where(core == 1, 1, 2))
    scalars = jnp.stack([z, pick_qv, pick_ko]).astype(jnp.int32)
    terms = layer_call(scalars, gathered, pack_second, [(q, q_x, q_d), (k, k_x, k_d), (v, v_x, v_d), (o, o_x, o_d)])
    summed = scatter_ring(*terms)
    keep = jnp.where(y == 0, summed[0], summed[1])
    give = jnp.where(y == 0, summed[1], summed[0]).astype(jnp.bfloat16)
    got = yswap(give)
    base = jnp.where(y == 0, stream[0], stream[1]).astype(jnp.float32)
    return (base + (keep + got.astype(jnp.float32))).astype(jnp.bfloat16)[None, None]


def solution(mesh):
    return jax.shard_map(
        per_device,
        mesh=mesh,
        in_specs=(
            P(None, "dp", "tensor", None),
            P("section", None),
            P("section", None, "tensor"),
            P("section", None, "tensor"),
            P("section", None, "tensor"),
            P("section", None, None),
            P("section", None, "tensor"),
            P("section", "tensor"),
            P("section", "tensor"),
            P("section", "tensor", None),
        ),
        out_specs=P("section", "dp", "tensor", None),
        check_vma=False,
    )
```

```python
import functools

import jax
import jax.numpy as jnp
from jax import lax
from jax.experimental import pallas as pl
from jax.experimental.pallas import tpu as pltpu
from jax.sharding import PartitionSpec as P

Z = 8
KEY = 64
VAL = 128
LEN = 256
RANK = 16
PACK = 40
OFFSETS = (0, 1, 2, 3, 5, 6, 7)


def zp(value):
    return lax.ppermute(value, "tensor", [(y * Z + z, y * Z + (z + 1) % Z) for y in range(2) for z in range(Z)])


def zm(value):
    return lax.ppermute(value, "tensor", [(y * Z + z, y * Z + (z + Z - 1) % Z) for y in range(2) for z in range(Z)])


def yswap(value):
    return lax.ppermute(value, "tensor", [(t, t ^ Z) for t in range(2 * Z)])


def to_second(value):
    n = 2 * Z
    return lax.ppermute(value, ("section", "tensor"), [(t, n + t) for t in range(n)])


def to_first(value):
    n = 2 * Z
    return lax.ppermute(value, ("section", "tensor"), [(n + t, t) for t in range(n)])


def to_sibling(value):
    return lax.ppermute(value, ("section", "dp"), [(d, d ^ 1) for d in range(lax.axis_size("dp"))])


def normalize(values, gain):
    return values * lax.rsqrt(jnp.mean(values * values, axis=-1, keepdims=True) + 1e-05) * gain


def gather_ring(block, midway=()):
    half = block.shape[0] // 2
    p1, m1 = zp(block), zm(block)
    p2, m2 = zp(p1), zm(m1)
    ready, *midway = lax.optimization_barrier((p2, *midway))
    p3, m3 = zp(ready), zm(m2)
    p4, m4 = zp(p3[:half]), zm(m3[half:])
    return ({0: block, 7: p1, 6: p2, 5: p3, 1: m1, 2: m2, 3: m3}, p4, m4), midway


def add(a, b):
    return (a.astype(jnp.float32) + b.astype(jnp.float32)).astype(jnp.bfloat16)


def scatter_ring(terms, four_a, four_b, early=(), midway=(), late=()):
    half = four_a.shape[0]
    four_a, *early = lax.optimization_barrier((four_a, *early))
    p, m = zp(four_a), zm(four_b)
    up = jnp.concatenate([add(terms[3][:half], p), terms[3][half:]], 0)
    down = jnp.concatenate([terms[5][:half], add(terms[5][half:], m)], 0)
    p, m = zp(up), zm(down)
    up, *midway = lax.optimization_barrier((add(terms[2], p), *midway))
    p, m = zp(up), zm(add(terms[6], m))
    up, *late = lax.optimization_barrier((add(terms[1], p), *late))
    p, m = zp(up), zm(add(terms[7], m))
    return terms[0].astype(jnp.float32) + p.astype(jnp.float32) + m.astype(jnp.float32), early, midway, late


def nt(a, b):
    return lax.dot_general(a, b, (((1,), (1,)), ((), ())), preferred_element_type=jnp.float32)


def mix(q, k, v, low, up, bias, gain):
    width = q.shape[1]
    heads = width // KEY
    half = LEN // 2
    logits = jnp.dot(low, up, preferred_element_type=jnp.float32) + bias
    log_sig = jnp.minimum(logits, 0.0) - jnp.log1p(jnp.exp(-jnp.abs(logits)))
    decay = jnp.exp(log_sig * (1.0 / 16.0))
    q = q.astype(jnp.float32) * KEY ** -0.5
    k = k.astype(jnp.float32)
    row = lax.broadcasted_iota(jnp.int32, (LEN, width), 0)
    lane_head = lax.broadcasted_iota(jnp.int32, (1, width), 1) // KEY
    head_masks = [jnp.where(lane_head == h, 1.0, 0.0).astype(jnp.bfloat16) for h in range(heads)]
    i = lax.broadcasted_iota(jnp.int32, (heads, half, half), 1)
    j = lax.broadcasted_iota(jnp.int32, (heads, half, half), 2)

    def scores(qb, kb, rows, columns):
        lhs = jnp.concatenate([qb[rows] * m for m in head_masks], axis=0)
        return nt(lhs, kb[columns]).reshape(heads, half, half)

    first, second = slice(0, half), slice(half, LEN)
    qb, kb = q.astype(jnp.bfloat16), k.astype(jnp.bfloat16)
    att = [jnp.where(i == j, scores(qb, kb, s, s), 0.0) for s in (first, second)]
    prefix, suffix, total = decay, jnp.ones_like(decay), decay
    b = 1
    while b < half:
        qb, kb = (q * prefix).astype(jnp.bfloat16), (k * suffix).astype(jnp.bfloat16)
        mask = ((i // (2 * b)) == (j // (2 * b))) & ((i & b) != 0) & ((j & b) == 0)
        att = [jnp.where(mask, scores(qb, kb, s, s), a) for s, a in zip((first, second), att)]
        upper = (row & b) != 0
        other = jnp.where(upper, pltpu.roll(total, b, 0), pltpu.roll(total, LEN - b, 0))
        prefix = jnp.where(upper, prefix * other, prefix)
        suffix = jnp.where(upper, suffix, suffix * other)
        total = total * other
        b *= 2
    qb, kb = (q * prefix).astype(jnp.bfloat16), (k * suffix).astype(jnp.bfloat16)
    across = scores(qb, kb, second, first)
    outs = []
    for h in range(heads):
        vh = v[:, h * VAL:(h + 1) * VAL]
        top = jnp.dot(att[0][h].astype(jnp.bfloat16), vh[first], preferred_element_type=jnp.float32)
        low_part = jnp.concatenate([across[h], att[1][h]], axis=1).astype(jnp.bfloat16)
        bottom = jnp.dot(low_part, vh, preferred_element_type=jnp.float32)
        mixed = jnp.concatenate([top, bottom], axis=0)
        scale = lax.rsqrt(jnp.maximum(jnp.mean(mixed * mixed, axis=-1, keepdims=True), 1.0))
        outs.append((mixed * scale * gain[:, h * VAL:(h + 1) * VAL]).astype(jnp.bfloat16))
    return jnp.concatenate(outs, axis=1)


def layer_kernel(groups, n_halves, scalars, *refs):
    at = 0

    def take(count):
        nonlocal at
        out = refs[at:at + count]
        at += count
        return out

    blocks = take(9)
    pack, q_src, k_src, v_src, o_src = take(5)
    halves = take(n_halves)
    outs = take(9)
    x, w, wo, y, gated, terms, sem = take(7)
    half = groups // 2
    z, fetched, core = scalars[0], scalars[1], scalars[2]
    depth = x.shape[2]
    wide = w.shape[2]

    sources = [(q_src, slice(None)), (k_src, slice(None)), (v_src, slice(0, wide)), (v_src, slice(wide, 2 * wide)),
               (o_src, slice(None))]
    targets = [w.at[0], w.at[1], w.at[2], w.at[3], wo]

    def own_copy(index):
        src, columns = sources[index]
        return pltpu.make_async_copy(src.at[:, columns], targets[index], sem.at[index])

    def start_own():
        for index in range(5):
            own_copy(index).start()

    def start_halves():
        for index in range(5):
            for n, side in ((0, core), (6, 1 - core)):
                parts = halves[n + index:n + index + 1] if index < 4 else halves[n + 4:n + 6]
                for m, src in enumerate(parts):
                    count = src.shape[0]
                    rows = pl.ds(pl.multiple_of((side * len(parts) + m) * count, count), count)
                    pltpu.make_async_copy(src, targets[index].at[rows, :], sem.at[index]).start()

    if n_halves:
        pl.when(fetched == 0)(start_own)
        pl.when(fetched == 1)(start_halves)
    else:
        start_own()

    def rows_of(offset):
        return pl.ds(pl.multiple_of(lax.rem(z + offset, Z) * 16, 16), 16)

    for n, offset in enumerate(OFFSETS):
        x[:, rows_of(offset), :] = blocks[n][...]
    x[0:half, rows_of(4), :] = blocks[7][...]
    x[half:groups, rows_of(4), :] = blocks[8][...]

    xs = x.reshape(groups * 128, depth)
    low = nt(xs[...], pack[0:RANK, :]).astype(jnp.bfloat16)
    for index in range(4):
        own_copy(index).wait()
        y[index] = jnp.dot(xs[...], w[index], preferred_element_type=jnp.float32).astype(jnp.bfloat16)
    gain = pack[17:18, 0:2 * wide].astype(jnp.float32)
    bias = sum(pack[r:r + 1, 0:wide].astype(jnp.float32) for r in (18, 19, 20))
    up = pack[24:24 + RANK, 0:wide]
    for n in range(groups // 2):
        s = slice(n * LEN, (n + 1) * LEN)
        v = jnp.concatenate([y[2, s, :], y[3, s, :]], axis=1)
        gated[s, :] = mix(y[0, s, :], y[1, s, :], v, low[s], up, bias, gain)
    own_copy(4).wait()
    step = 512
    for c in range(depth // step):
        cols = slice(c * step, (c + 1) * step)
        part = jnp.dot(gated[...], wo[:, cols], preferred_element_type=jnp.float32).astype(jnp.bfloat16)
        part = part.reshape(groups, Z, 16, step)
        for to in range(Z):
            terms[lax.rem(to - z + Z, Z), :, :, cols] = part[:, to]
    for n, offset in enumerate(OFFSETS):
        outs[n][...] = terms[offset]
    outs[7][...] = terms[4, 0:half]
    outs[8][...] = terms[4, half:groups]


def layer_call(scalars, gathered, pack, weights, halves=()):
    by_offset, p4, m4 = gathered
    groups, _, depth = by_offset[0].shape
    count = groups * 128
    bf = jnp.bfloat16
    part = jax.ShapeDtypeStruct((groups // 2, 16, depth), bf)
    anywhere = pl.BlockSpec(memory_space=pl.ANY)
    vmem = pl.BlockSpec(memory_space=pltpu.VMEM)
    wide = weights[0].shape[1]
    operands = [by_offset[o] for o in OFFSETS] + [p4, m4, pack, *weights, *halves]
    outs = pl.pallas_call(
        functools.partial(layer_kernel, groups, len(halves)),
        out_shape=[jax.ShapeDtypeStruct((groups, 16, depth), bf)] * 7 + [part] * 2,
        in_specs=[pl.BlockSpec(memory_space=pltpu.SMEM)] + [vmem] * 10 + [anywhere] * (4 + len(halves)),
        out_specs=[vmem] * 9,
        scratch_shapes=[
            pltpu.VMEM((groups, 128, depth), bf),
            pltpu.VMEM((4, depth, wide), bf),
            pltpu.VMEM((2 * wide, depth), bf),
            pltpu.VMEM((4, count, wide), bf),
            pltpu.VMEM((count, 2 * wide), bf),
            pltpu.VMEM((Z, groups, 16, depth), bf),
            pltpu.SemaphoreType.DMA((5,)),
        ],
        compiler_params=pltpu.CompilerParams(vmem_limit_bytes=40 * 1024 * 1024),
        cost_estimate=pl.CostEstimate(flops=count * depth, bytes_accessed=count * depth, transcendentals=0),
    )(scalars, *operands)
    return dict(zip(OFFSETS, outs[:7])), outs[7], outs[8]


def make_pack(norm_gain, decay_down, decay_up, decay_bias, head_gain):
    depth = norm_gain.shape[0]

    def wide(rows):
        return jnp.pad(rows.astype(jnp.bfloat16), ((0, 0), (0, depth - rows.shape[1])))

    high = lax.reduce_precision(decay_bias, 8, 7)
    middle = lax.reduce_precision(decay_bias - high, 8, 7)
    bias = jnp.stack([high, middle, decay_bias - high - middle])
    return jnp.concatenate([
        decay_down.T, norm_gain[None], wide(head_gain[None]), wide(bias),
        jnp.zeros((24 - RANK - 5, depth), jnp.bfloat16), wide(decay_up),
    ], axis=0)


def per_device(activations, norm_gain, query_matrix, key_weight, value_weight, decay_down, decay_up,
               decay_bias, head_gain, output_matrix):
    section = lax.axis_index("section")
    core = lax.axis_index("dp") % 2
    tensor = lax.axis_index("tensor")
    y, z = tensor // Z, tensor % Z
    q, k, v, o = query_matrix[0], key_weight[0], value_weight[0], output_matrix[0]
    pack = make_pack(norm_gain[0], decay_down[0], decay_up[0], decay_bias[0], head_gain[0])

    def half_of(rows):
        return lax.dynamic_slice_in_dim(rows, core * (rows.shape[0] // 2), rows.shape[0] // 2, 0)

    wide = q.shape[1]
    pieces = [half_of(q), half_of(k), half_of(v[:, :wide]), half_of(v[:, wide:])]
    o_half = half_of(o)
    pieces += [o_half[:wide // 2], o_half[wide // 2:]]
    pack_x = to_first(pack)
    crossed = [to_first(piece) for piece in pieces]

    mine = activations[:, 0]
    other = yswap(mine)
    pair = jnp.stack([jnp.where(y == 0, mine, other), jnp.where(y == 0, other, mine)], axis=1)
    normed = normalize(pair.astype(jnp.float32), norm_gain[0].astype(jnp.float32)).astype(jnp.bfloat16)
    gathered, (crossed[0],) = gather_ring(normed.reshape(4, 16, -1), (crossed[0],))
    zero = jnp.zeros((), jnp.int32)
    scalars = jnp.stack([z, zero, zero]).astype(jnp.int32)
    scalars, crossed[1] = lax.optimization_barrier((scalars, crossed[1]))
    terms = layer_call(scalars, gathered, pack, (q, k, v, o))
    summed, (crossed[2],), (crossed[3],), (crossed[4],) = scatter_ring(
        *terms, (crossed[2],), (crossed[3],), (crossed[4],))
    summed = summed.astype(jnp.bfloat16).reshape(2, 2, 16, -1)
    summed, pack_x = lax.optimization_barrier((summed, pack_x))
    sibling = [to_sibling(piece) for piece in crossed]

    own = jnp.where(section == 0, summed[0], to_second(summed[1]))
    partner = yswap(own)
    stream = jnp.where(section == 0, pair[0], pair[1]).astype(jnp.float32)
    stream = (stream + (own.astype(jnp.float32) + partner.astype(jnp.float32))).astype(jnp.bfloat16)
    pack_second = jnp.where(section == 0, pack_x, pack)
    normed = normalize(stream.astype(jnp.float32), pack_second[RANK].astype(jnp.float32)).astype(jnp.bfloat16)
    normed, *sibling[:5] = lax.optimization_barrier((normed, *sibling[:5]))
    gathered, _ = gather_ring(normed)
    scalars = jnp.stack([z, 1 - section, core]).astype(jnp.int32)
    terms = layer_call(scalars, gathered, pack_second, (q, k, v, o), (*crossed, *sibling))
    summed, *_ = scatter_ring(*terms)
    keep = jnp.where(y == 0, summed[0], summed[1])
    give = jnp.where(y == 0, summed[1], summed[0]).astype(jnp.bfloat16)
    got = yswap(give)
    base = jnp.where(y == 0, stream[0], stream[1]).astype(jnp.float32)
    return (base + (keep + got.astype(jnp.float32))).astype(jnp.bfloat16)[None, None]


def solution(mesh):
    return jax.shard_map(
        per_device,
        mesh=mesh,
        in_specs=(
            P(None, "dp", "tensor", None),
            P("section", None),
            P("section", None, "tensor"),
            P("section", None, "tensor"),
            P("section", None, "tensor"),
            P("section", None, None),
            P("section", None, "tensor"),
            P("section", "tensor"),
            P("section", "tensor"),
            P("section", "tensor", None),
        ),
        out_specs=P("section", "dp", "tensor", None),
        check_vma=False,
    )
```

```python
import functools

import jax
import jax.numpy as jnp
from jax import lax
from jax.experimental import pallas as pl
from jax.experimental.pallas import tpu as pltpu
from jax.sharding import PartitionSpec as P

Z = 8
KEY = 64
VAL = 128
LEN = 256
RANK = 16
PACK = 40
OFFSETS = (0, 1, 2, 3, 5, 6, 7)


def zp(value):
    return lax.ppermute(value, "tensor", [(y * Z + z, y * Z + (z + 1) % Z) for y in range(2) for z in range(Z)])


def zm(value):
    return lax.ppermute(value, "tensor", [(y * Z + z, y * Z + (z + Z - 1) % Z) for y in range(2) for z in range(Z)])


def yswap(value):
    return lax.ppermute(value, "tensor", [(t, t ^ Z) for t in range(2 * Z)])


def to_second(value):
    n = 2 * Z
    return lax.ppermute(value, ("section", "tensor"), [(t, n + t) for t in range(n)])


def to_first(value):
    n = 2 * Z
    return lax.ppermute(value, ("section", "tensor"), [(n + t, t) for t in range(n)])


def to_sibling(value):
    return lax.ppermute(value, ("section", "dp"), [(d, d ^ 1) for d in range(lax.axis_size("dp"))])


def normalize(values, gain):
    return values * lax.rsqrt(jnp.mean(values * values, axis=-1, keepdims=True) + 1e-05) * gain


def hold(value, far, names):
    if names:
        value, *arrived = lax.optimization_barrier((value, *[far[n] for n in names]))
        far.update(zip(names, arrived))
    return value


def gather_ring(block, far, at):
    half = block.shape[0] // 2
    p1, m1 = zp(block), zm(block)
    p2, m2 = zp(hold(p1, far, at.get(2))), zm(m1)
    p3, m3 = zp(hold(p2, far, at.get(3))), zm(m2)
    p4, m4 = zp(hold(p3[:half], far, at.get(4))), zm(m3[half:])
    return {0: block, 7: p1, 6: p2, 5: p3, 1: m1, 2: m2, 3: m3}, p4, m4


def add(a, b):
    return (a.astype(jnp.float32) + b.astype(jnp.float32)).astype(jnp.bfloat16)


def scatter_ring(terms, four_a, four_b, far, at):
    half = four_a.shape[0]
    p, m = zp(four_a), zm(four_b)
    up = jnp.concatenate([add(terms[3][:half], p), terms[3][half:]], 0)
    down = jnp.concatenate([terms[5][:half], add(terms[5][half:], m)], 0)
    p, m = zp(hold(up, far, at.get(2))), zm(down)
    p, m = zp(hold(add(terms[2], p), far, at.get(3))), zm(add(terms[6], m))
    p, m = zp(hold(add(terms[1], p), far, at.get(4))), zm(add(terms[7], m))
    return terms[0].astype(jnp.float32) + p.astype(jnp.float32) + m.astype(jnp.float32)


def nt(a, b):
    return lax.dot_general(a, b, (((1,), (1,)), ((), ())), preferred_element_type=jnp.float32)


def mix(q, k, v, low, up, bias, gain):
    width = q.shape[1]
    heads = width // KEY
    half = LEN // 2
    logits = jnp.dot(low, up, preferred_element_type=jnp.float32) + bias
    log_sig = jnp.minimum(logits, 0.0) - jnp.log1p(jnp.exp(-jnp.abs(logits)))
    decay = jnp.exp(log_sig * (1.0 / 16.0))
    q = q.astype(jnp.float32) * KEY ** -0.5
    k = k.astype(jnp.float32)
    row = lax.broadcasted_iota(jnp.int32, (LEN, width), 0)
    lane_head = lax.broadcasted_iota(jnp.int32, (1, width), 1) // KEY
    head_masks = [jnp.where(lane_head == h, 1.0, 0.0).astype(jnp.bfloat16) for h in range(heads)]
    i = lax.broadcasted_iota(jnp.int32, (heads, half, half), 1)
    j = lax.broadcasted_iota(jnp.int32, (heads, half, half), 2)

    def scores(qb, kb, rows, columns):
        lhs = jnp.concatenate([qb[rows] * m for m in head_masks], axis=0)
        return nt(lhs, kb[columns]).reshape(heads, half, half)

    first, second = slice(0, half), slice(half, LEN)
    qb, kb = q.astype(jnp.bfloat16), k.astype(jnp.bfloat16)
    att = [jnp.where(i == j, scores(qb, kb, s, s), 0.0) for s in (first, second)]
    prefix, suffix, total = decay, jnp.ones_like(decay), decay
    b = 1
    while b < half:
        qb, kb = (q * prefix).astype(jnp.bfloat16), (k * suffix).astype(jnp.bfloat16)
        mask = ((i // (2 * b)) == (j // (2 * b))) & ((i & b) != 0) & ((j & b) == 0)
        att = [jnp.where(mask, scores(qb, kb, s, s), a) for s, a in zip((first, second), att)]
        upper = (row & b) != 0
        other = jnp.where(upper, pltpu.roll(total, b, 0), pltpu.roll(total, LEN - b, 0))
        prefix = jnp.where(upper, prefix * other, prefix)
        suffix = jnp.where(upper, suffix, suffix * other)
        total = total * other
        b *= 2
    qb, kb = (q * prefix).astype(jnp.bfloat16), (k * suffix).astype(jnp.bfloat16)
    across = scores(qb, kb, second, first)
    outs = []
    for h in range(heads):
        vh = v[:, h * VAL:(h + 1) * VAL]
        top = jnp.dot(att[0][h].astype(jnp.bfloat16), vh[first], preferred_element_type=jnp.float32)
        low_part = jnp.concatenate([across[h], att[1][h]], axis=1).astype(jnp.bfloat16)
        bottom = jnp.dot(low_part, vh, preferred_element_type=jnp.float32)
        mixed = jnp.concatenate([top, bottom], axis=0)
        scale = lax.rsqrt(jnp.maximum(jnp.mean(mixed * mixed, axis=-1, keepdims=True), 1.0))
        outs.append((mixed * scale * gain[:, h * VAL:(h + 1) * VAL]).astype(jnp.bfloat16))
    return jnp.concatenate(outs, axis=1)


def layer_kernel(groups, n_halves, scalars, *refs):
    at = 0

    def take(count):
        nonlocal at
        out = refs[at:at + count]
        at += count
        return out

    blocks = take(9)
    pack, q_src, k_src, v_src, o_src = take(5)
    halves = take(n_halves)
    outs = take(9)
    x, w, wo, y, gated, terms, sem = take(7)
    half = groups // 2
    z, fetched, core = scalars[0], scalars[1], scalars[2]
    depth = x.shape[2]
    wide = w.shape[2]

    sources = [(q_src, slice(None)), (k_src, slice(None)), (v_src, slice(0, wide)), (v_src, slice(wide, 2 * wide)),
               (o_src, slice(None))]
    targets = [w.at[0], w.at[1], w.at[2], w.at[3], wo]

    def own_copy(index):
        src, columns = sources[index]
        return pltpu.make_async_copy(src.at[:, columns], targets[index], sem.at[index])

    def start_own():
        for index in range(5):
            own_copy(index).start()

    def copy_halves():
        for (qkv, v, *o), side in ((halves[0:4], core), (halves[4:8], 1 - core)):
            rows = pl.ds(pl.multiple_of(side * (depth // 2), depth // 2), depth // 2)
            most = wide // 2
            w[0, rows, :] = qkv[:, 0:wide]
            w[1, rows, :] = qkv[:, wide:2 * wide]
            w[2, rows, 0:most] = qkv[:, 2 * wide:]
            w[2, rows, most:] = v[:, 0:most]
            w[3, rows, :] = v[:, most:]
            for n in range(2):
                wo[pl.ds(pl.multiple_of(side * wide + n * most, most), most), :] = o[n][...]

    if n_halves:
        pl.when(fetched == 0)(start_own)
        pl.when(fetched == 1)(copy_halves)
    else:
        start_own()

    def rows_of(offset):
        return pl.ds(pl.multiple_of(lax.rem(z + offset, Z) * 16, 16), 16)

    for n, offset in enumerate(OFFSETS):
        x[:, rows_of(offset), :] = blocks[n][...]
    x[0:half, rows_of(4), :] = blocks[7][...]
    x[half:groups, rows_of(4), :] = blocks[8][...]

    xs = x.reshape(groups * 128, depth)
    low = nt(xs[...], pack[0:RANK, :]).astype(jnp.bfloat16)

    def wait(index):
        if n_halves:
            pl.when(fetched == 0)(own_copy(index).wait)
        else:
            own_copy(index).wait()

    for index in range(4):
        wait(index)
        y[index] = jnp.dot(xs[...], w[index], preferred_element_type=jnp.float32).astype(jnp.bfloat16)
    gain = pack[17:18, 0:2 * wide].astype(jnp.float32)
    bias = sum(pack[r:r + 1, 0:wide].astype(jnp.float32) for r in (18, 19, 20))
    up = pack[24:24 + RANK, 0:wide]
    for n in range(groups // 2):
        s = slice(n * LEN, (n + 1) * LEN)
        v = jnp.concatenate([y[2, s, :], y[3, s, :]], axis=1)
        gated[s, :] = mix(y[0, s, :], y[1, s, :], v, low[s], up, bias, gain)
    wait(4)
    step = 512
    for c in range(depth // step):
        cols = slice(c * step, (c + 1) * step)
        part = jnp.dot(gated[...], wo[:, cols], preferred_element_type=jnp.float32).astype(jnp.bfloat16)
        part = part.reshape(groups, Z, 16, step)
        for to in range(Z):
            terms[lax.rem(to - z + Z, Z), :, :, cols] = part[:, to]
    for n, offset in enumerate(OFFSETS):
        outs[n][...] = terms[offset]
    outs[7][...] = terms[4, 0:half]
    outs[8][...] = terms[4, half:groups]


def layer_call(scalars, gathered, pack, weights, halves=()):
    by_offset, p4, m4 = gathered
    groups, _, depth = by_offset[0].shape
    count = groups * 128
    bf = jnp.bfloat16
    part = jax.ShapeDtypeStruct((groups // 2, 16, depth), bf)
    anywhere = pl.BlockSpec(memory_space=pl.ANY)
    vmem = pl.BlockSpec(memory_space=pltpu.VMEM)
    wide = weights[0].shape[1]
    operands = [by_offset[o] for o in OFFSETS] + [p4, m4, pack, *weights, *halves]
    outs = pl.pallas_call(
        functools.partial(layer_kernel, groups, len(halves)),
        out_shape=[jax.ShapeDtypeStruct((groups, 16, depth), bf)] * 7 + [part] * 2,
        in_specs=[pl.BlockSpec(memory_space=pltpu.SMEM)] + [vmem] * 10 + [anywhere] * 4 + [vmem] * len(halves),
        out_specs=[vmem] * 9,
        scratch_shapes=[
            pltpu.VMEM((groups, 128, depth), bf),
            pltpu.VMEM((4, depth, wide), bf),
            pltpu.VMEM((2 * wide, depth), bf),
            pltpu.VMEM((4, count, wide), bf),
            pltpu.VMEM((count, 2 * wide), bf),
            pltpu.VMEM((Z, groups, 16, depth), bf),
            pltpu.SemaphoreType.DMA((5,)),
        ],
        compiler_params=pltpu.CompilerParams(vmem_limit_bytes=40 * 1024 * 1024),
        cost_estimate=pl.CostEstimate(flops=count * depth, bytes_accessed=count * depth, transcendentals=0),
    )(scalars, *operands)
    return dict(zip(OFFSETS, outs[:7])), outs[7], outs[8]


def make_pack(norm_gain, decay_down, decay_up, decay_bias, head_gain):
    depth = norm_gain.shape[0]

    def wide(rows):
        return jnp.pad(rows.astype(jnp.bfloat16), ((0, 0), (0, depth - rows.shape[1])))

    high = lax.reduce_precision(decay_bias, 8, 7)
    middle = lax.reduce_precision(decay_bias - high, 8, 7)
    bias = jnp.stack([high, middle, decay_bias - high - middle])
    return jnp.concatenate([
        decay_down.T, norm_gain[None], wide(head_gain[None]), wide(bias),
        jnp.zeros((24 - RANK - 5, depth), jnp.bfloat16), wide(decay_up),
    ], axis=0)


def per_device(activations, norm_gain, query_matrix, key_weight, value_weight, decay_down, decay_up,
               decay_bias, head_gain, output_matrix):
    section = lax.axis_index("section")
    core = lax.axis_index("dp") % 2
    tensor = lax.axis_index("tensor")
    y, z = tensor // Z, tensor % Z
    q, k, v, o = query_matrix[0], key_weight[0], value_weight[0], output_matrix[0]
    pack = make_pack(norm_gain[0], decay_down[0], decay_up[0], decay_bias[0], head_gain[0])

    def half_of(rows):
        return lax.dynamic_slice_in_dim(rows, core * (rows.shape[0] // 2), rows.shape[0] // 2, 0)

    most = v.shape[1] // 4
    o_half = half_of(o)
    rest = o_half.shape[0] // 2
    far = {
        "a": jnp.concatenate([half_of(q), half_of(k), half_of(v[:, :most])], axis=1),
        "b": half_of(v[:, most:]),
        "c": o_half[:rest],
        "d": o_half[rest:],
        "pack": pack,
    }
    far = {n: to_first(value) for n, value in far.items()}
    for n in "abcd":
        far[n + "2"] = to_sibling(far[n])

    mine = activations[:, 0]
    other = yswap(mine)
    pair = jnp.stack([jnp.where(y == 0, mine, other), jnp.where(y == 0, other, mine)], axis=1)
    normed = normalize(pair.astype(jnp.float32), norm_gain[0].astype(jnp.float32)).astype(jnp.bfloat16)
    gathered = gather_ring(normed.reshape(4, 16, -1), far, {4: ["a"]})
    zero = jnp.zeros((), jnp.int32)
    scalars = jnp.stack([z, zero, zero]).astype(jnp.int32)
    terms, four_a, four_b = layer_call(scalars, gathered, pack, (q, k, v, o))
    four_a = hold(four_a, far, ["b"])
    summed = scatter_ring(terms, four_a, four_b, far, {2: ["a2"], 3: ["c"], 4: ["b2", "d"]})
    summed = hold(summed.astype(jnp.bfloat16).reshape(2, 2, 16, -1), far, ["c2", "pack"])

    own = jnp.where(section == 0, summed[0], to_second(summed[1]))
    partner = yswap(own)
    stream = jnp.where(section == 0, pair[0], pair[1]).astype(jnp.float32)
    stream = (stream + (own.astype(jnp.float32) + partner.astype(jnp.float32))).astype(jnp.bfloat16)
    pack_second = jnp.where(section == 0, far["pack"], pack)
    normed = normalize(stream.astype(jnp.float32), pack_second[RANK].astype(jnp.float32)).astype(jnp.bfloat16)
    gathered = gather_ring(normed, far, {3: ["d2"]})
    scalars = jnp.stack([z, 1 - section, core]).astype(jnp.int32)
    terms = layer_call(scalars, gathered, pack_second, (q, k, v, o), [far[n] for n in ("a", "b", "c", "d", "a2", "b2", "c2", "d2")])
    summed = scatter_ring(*terms, far, {})
    keep = jnp.where(y == 0, summed[0], summed[1])
    give = jnp.where(y == 0, summed[1], summed[0]).astype(jnp.bfloat16)
    got = yswap(give)
    base = jnp.where(y == 0, stream[0], stream[1]).astype(jnp.float32)
    return (base + (keep + got.astype(jnp.float32))).astype(jnp.bfloat16)[None, None]


def solution(mesh):
    return jax.shard_map(
        per_device,
        mesh=mesh,
        in_specs=(
            P(None, "dp", "tensor", None),
            P("section", None),
            P("section", None, "tensor"),
            P("section", None, "tensor"),
            P("section", None, "tensor"),
            P("section", None, None),
            P("section", None, "tensor"),
            P("section", "tensor"),
            P("section", "tensor"),
            P("section", "tensor", None),
        ),
        out_specs=P("section", "dp", "tensor", None),
        check_vma=False,
    )
```

```python
import functools

import jax
import jax.numpy as jnp
from jax import lax
from jax.experimental import pallas as pl
from jax.experimental.pallas import tpu as pltpu
from jax.sharding import PartitionSpec as P

Z = 8
KEY = 64
VAL = 128
LEN = 256
RANK = 16
PACK = 40
OFFSETS = (0, 1, 2, 3, 5, 6, 7)


def ring(value, by, sections):
    pairs = [(s * 2 * Z + y * Z + z, s * 2 * Z + y * Z + (z + by) % Z)
             for s in sections for y in range(2) for z in range(Z)]
    return lax.ppermute(value, ("section", "tensor"), pairs)


def yswap(value):
    return lax.ppermute(value, "tensor", [(t, t ^ Z) for t in range(2 * Z)])


def to_second(value):
    n = 2 * Z
    return lax.ppermute(value, ("section", "tensor"), [(t, n + t) for t in range(n)])


def to_first(value):
    n = 2 * Z
    return lax.ppermute(value, ("section", "tensor"), [(n + t, t) for t in range(n)])


def to_sibling(value):
    return lax.ppermute(value, ("section", "dp"), [(d, d ^ 1) for d in range(lax.axis_size("dp"))])


def normalize(values, gain):
    return values * lax.rsqrt(jnp.mean(values * values, axis=-1, keepdims=True) + 1e-05) * gain


def hold(value, far, names):
    if names:
        value, *arrived = lax.optimization_barrier((value, *[far[n] for n in names]))
        far.update(zip(names, arrived))
    return value


def gather_ring(block, z, sections, far, at):
    zp = functools.partial(ring, by=1, sections=sections)
    zm = functools.partial(ring, by=Z - 1, sections=sections)
    groups, size, depth = block.shape
    half = groups // 2

    def place(x, block, offset, first=0):
        return lax.dynamic_update_slice(x, block, (first, (z + offset) % Z * size, 0))

    p, m = zp(block), zm(block)
    x = place(jnp.zeros((groups, Z * size, depth), block.dtype), block, 0)
    for step in (2, 3):
        x = place(place(x, p, Z + 1 - step), m, step - 1)
        p, m = zp(hold(p, far, at.get(step))), zm(m)
    x = place(place(x, p, Z - 3), m, 3)
    p, m = zp(hold(p[:half], far, at.get(4))), zm(m[half:])
    return place(place(x, p, 4), m, 4, half)


def add(a, b):
    return (a.astype(jnp.float32) + b.astype(jnp.float32)).astype(jnp.bfloat16)


def scatter_ring(terms, four_a, four_b, sections, far, at):
    zp = functools.partial(ring, by=1, sections=sections)
    zm = functools.partial(ring, by=Z - 1, sections=sections)
    half = four_a.shape[0]
    p, m = zp(four_a), zm(four_b)
    up = jnp.concatenate([add(terms[3][:half], p), terms[3][half:]], 0)
    down = jnp.concatenate([terms[5][:half], add(terms[5][half:], m)], 0)
    p, m = zp(hold(up, far, at.get(2))), zm(down)
    p, m = zp(hold(add(terms[2], p), far, at.get(3))), zm(add(terms[6], m))
    p, m = zp(hold(add(terms[1], p), far, at.get(4))), zm(add(terms[7], m))
    return terms[0].astype(jnp.float32) + p.astype(jnp.float32) + m.astype(jnp.float32)


def nt(a, b):
    return lax.dot_general(a, b, (((1,), (1,)), ((), ())), preferred_element_type=jnp.float32)


def mix(q, k, v, low, up, bias, gain):
    width = q.shape[1]
    heads = width // KEY
    half = LEN // 2
    bf = jnp.bfloat16
    logits = jnp.dot(low, up, preferred_element_type=jnp.float32) + bias
    log_sig = jnp.minimum(logits, 0.0) - jnp.log(1.0 + jnp.exp(-jnp.abs(logits)))
    decay = jnp.exp(log_sig * (1.0 / 16.0))
    q = q.astype(jnp.float32) * KEY ** -0.5
    row = lax.broadcasted_iota(jnp.int32, (LEN, width), 0)
    lane_head = lax.broadcasted_iota(jnp.int32, (1, width), 1) // KEY
    head_masks = [jnp.where(lane_head == h, 1.0, 0.0).astype(bf) for h in range(heads)]
    i = lax.broadcasted_iota(jnp.int32, (half, half), 0)
    j = lax.broadcasted_iota(jnp.int32, (half, half), 1)
    apart = jnp.where(i > j, i ^ j, 0)
    first, second = slice(0, half), slice(half, LEN)

    def scores(qb, kb):
        lhs = jnp.concatenate([qb * m for m in head_masks], axis=0)
        return nt(lhs, kb).reshape(heads, qb.shape[0], half)

    qb = q.astype(bf)
    att = [jnp.where((i == j)[None], scores(qb[s], k[s]), 0.0) for s in (first, second)]
    q, k, total = q * decay, k.astype(jnp.float32), decay
    for level in range(3):
        b = 1 << level
        qb, kb = q.astype(bf), k.astype(bf)
        mask = ((apart >> level) == 1)[None]
        att = [jnp.where(mask, scores(qb[s], kb[s]), a) for s, a in zip((first, second), att)]
        upper = (row & b) != 0
        other = jnp.where(upper, pltpu.roll(total, b, 0), pltpu.roll(total, LEN - b, 0))
        q = jnp.where(upper, q * other, q)
        k = jnp.where(upper, k, k * other)
        total = total * other
    total = total.reshape(LEN // 8, 8, width)
    for level in range(3, 7):
        b = 1 << level
        pairs = half // (2 * b)
        kb = k.astype(bf)
        q = q.reshape(2 * pairs, 2, b, width)
        qb = q[:, 1].astype(bf).reshape(2, half // 2, width)
        mask = ((apart >> level) == 1).astype(jnp.int32).reshape(pairs, 2, b, half)[:, 1] == 1
        for n, s in enumerate((first, second)):
            a = att[n].reshape(heads, pairs, 2, b, half)
            upper = jnp.where(mask[None], scores(qb[n], kb[s]).reshape(heads, pairs, b, half), a[:, :, 1])
            att[n] = jnp.stack([a[:, :, 0], upper], axis=2).reshape(heads, half, half)
        total = total.reshape(2 * pairs, 2, 1, 8, width)
        begins, ends = total[:, 0], total[:, 1]
        upper = (q[:, 1].reshape(2 * pairs, b // 8, 8, width) * begins).reshape(2 * pairs, b, width)
        q = jnp.stack([q[:, 0], upper], axis=1).reshape(LEN, width)
        k = k.reshape(2 * pairs, 2, b, width)
        lower = (k[:, 0].reshape(2 * pairs, b // 8, 8, width) * ends).reshape(2 * pairs, b, width)
        k = jnp.stack([lower, k[:, 1]], axis=1).reshape(LEN, width)
        total = begins * ends
    across = scores(q[second].astype(bf), k[first].astype(bf))
    outs = []
    for h in range(heads):
        vh = v[:, h * VAL:(h + 1) * VAL]
        top = jnp.dot(att[0][h].astype(bf), vh[first], preferred_element_type=jnp.float32)
        bottom = jnp.dot(jnp.concatenate([across[h], att[1][h]], axis=1).astype(bf), vh,
                         preferred_element_type=jnp.float32)
        mixed = jnp.concatenate([top, bottom], axis=0)
        scale = lax.rsqrt(jnp.maximum(jnp.mean(mixed * mixed, axis=-1, keepdims=True), 1.0))
        outs.append((mixed * scale * gain[:, h * VAL:(h + 1) * VAL]).astype(bf))
    return jnp.concatenate(outs, axis=1)


def layer_kernel(groups, n_halves, scalars, *refs):
    at = 0

    def take(count):
        nonlocal at
        out = refs[at:at + count]
        at += count
        return out

    x, pack, q_src, k_src, v_src, o_src = take(6)
    halves = take(n_halves)
    outs = take(9)
    w, wo, y, gated, sem = take(5)
    half = groups // 2
    z, fetched, core = scalars[0], scalars[1], scalars[2]
    depth = x.shape[1]
    wide = w.shape[2]

    sources = [(q_src, slice(None)), (k_src, slice(None)), (v_src, slice(0, wide)), (v_src, slice(wide, 2 * wide)),
               (o_src, slice(None))]
    targets = [w.at[0], w.at[1], w.at[2], w.at[3], wo]

    def own_copy(index):
        src, columns = sources[index]
        return pltpu.make_async_copy(src.at[:, columns], targets[index], sem.at[index])

    def start_own():
        for index in range(5):
            own_copy(index).start()

    def start_halves():
        most = wide // 2
        for (a, b, c, d), side in ((halves[0:4], core), (halves[4:8], 1 - core)):
            rows = pl.ds(pl.multiple_of(side * (depth // 2), depth // 2), depth // 2)
            low_rows = pl.ds(pl.multiple_of(side * wide, wide), most)
            high_rows = pl.ds(pl.multiple_of(side * wide + most, most), most)
            for index, src, dst in (
                (0, a.at[:, 0:wide], w.at[0, rows, :]),
                (1, a.at[:, wide:2 * wide], w.at[1, rows, :]),
                (2, a.at[:, 2 * wide:], w.at[2, rows, 0:most]),
                (2, b.at[:, 0:most], w.at[2, rows, most:]),
                (3, b.at[:, most:], w.at[3, rows, :]),
                (4, c, wo.at[low_rows, :]),
                (4, d, wo.at[high_rows, :]),
            ):
                pltpu.make_async_copy(src, dst, sem.at[index]).start()

    if n_halves:
        pl.when(fetched == 0)(start_own)
        pl.when(fetched == 1)(start_halves)
    else:
        start_own()

    low = nt(x[...], pack[0:RANK, :]).astype(jnp.bfloat16)

    for index in range(4):
        own_copy(index).wait()
        y[index] = jnp.dot(x[...], w[index], preferred_element_type=jnp.float32).astype(jnp.bfloat16)
    gain = pack[17:18, 0:2 * wide].astype(jnp.float32)
    bias = sum(pack[r:r + 1, 0:wide].astype(jnp.float32) for r in (18, 19, 20))
    up = pack[24:24 + RANK, 0:wide]
    for n in range(groups // 2):
        s = slice(n * LEN, (n + 1) * LEN)
        v = jnp.concatenate([y[2, s, :], y[3, s, :]], axis=1)
        mixed = mix(y[0, s, :], y[1, s, :], v, low[s], up, bias, gain)
        for g in range(2):
            for to in range(Z):
                at = pl.multiple_of((lax.rem(to - z + Z, Z) * groups + 2 * n + g) * 16, 16)
                gated[pl.ds(at, 16), :] = mixed[g * 128 + to * 16:g * 128 + to * 16 + 16]
    own_copy(4).wait()
    step = 512
    for c in range(depth // step):
        cols = slice(c * step, (c + 1) * step)
        part = jnp.dot(gated[...], wo[:, cols], preferred_element_type=jnp.float32).astype(jnp.bfloat16)
        part = part.reshape(Z, groups, 16, step)
        for n, offset in enumerate(OFFSETS):
            outs[n][:, :, cols] = part[offset]
        outs[7][:, :, cols] = part[4, 0:half]
        outs[8][:, :, cols] = part[4, half:groups]


def layer_call(scalars, gathered, pack, weights, halves=()):
    groups, _, depth = gathered.shape
    count = groups * 128
    bf = jnp.bfloat16
    part = jax.ShapeDtypeStruct((groups // 2, 16, depth), bf)
    hbm = pl.BlockSpec(memory_space=pltpu.HBM)
    vmem = pl.BlockSpec(memory_space=pltpu.VMEM)
    wide = weights[0].shape[1]
    operands = [gathered.reshape(count, depth), pack, *weights, *halves]
    outs = pl.pallas_call(
        functools.partial(layer_kernel, groups, len(halves)),
        out_shape=[jax.ShapeDtypeStruct((groups, 16, depth), bf)] * 7 + [part] * 2,
        in_specs=[pl.BlockSpec(memory_space=pltpu.SMEM)] + [vmem] * 2 + [hbm] * (4 + len(halves)),
        out_specs=[vmem] * 9,
        scratch_shapes=[
            pltpu.VMEM((4, depth, wide), bf),
            pltpu.VMEM((2 * wide, depth), bf),
            pltpu.VMEM((4, count, wide), bf),
            pltpu.VMEM((count, 2 * wide), bf),
            pltpu.SemaphoreType.DMA((5,)),
        ],
        compiler_params=pltpu.CompilerParams(vmem_limit_bytes=50 * 1024 * 1024),
        cost_estimate=pl.CostEstimate(flops=count * depth, bytes_accessed=count * depth, transcendentals=0),
    )(scalars, *operands)
    return dict(zip(OFFSETS, outs[:7])), outs[7], outs[8]


def make_pack(norm_gain, decay_down, decay_up, decay_bias, head_gain):
    depth = norm_gain.shape[0]

    def wide(rows):
        return jnp.pad(rows.astype(jnp.bfloat16), ((0, 0), (0, depth - rows.shape[1])))

    high = lax.reduce_precision(decay_bias, 8, 7)
    middle = lax.reduce_precision(decay_bias - high, 8, 7)
    bias = jnp.stack([high, middle, decay_bias - high - middle])
    return jnp.concatenate([
        decay_down.T, norm_gain[None], wide(head_gain[None]), wide(bias),
        jnp.zeros((24 - RANK - 5, depth), jnp.bfloat16), wide(decay_up),
    ], axis=0)


def per_device(activations, norm_gain, query_matrix, key_weight, value_weight, decay_down, decay_up,
               decay_bias, head_gain, output_matrix):
    section = lax.axis_index("section")
    core = lax.axis_index("dp") % 2
    tensor = lax.axis_index("tensor")
    y, z = tensor // Z, tensor % Z
    q, k, v, o = query_matrix[0], key_weight[0], value_weight[0], output_matrix[0]
    pack = make_pack(norm_gain[0], decay_down[0], decay_up[0], decay_bias[0], head_gain[0])

    def half_of(rows):
        return lax.dynamic_slice_in_dim(rows, core * (rows.shape[0] // 2), rows.shape[0] // 2, 0)

    most = v.shape[1] // 4
    o_half = half_of(o)
    rest = o_half.shape[0] // 2
    far = {
        "a": jnp.concatenate([half_of(q), half_of(k), half_of(v[:, :most])], axis=1),
        "b": half_of(v[:, most:]),
        "c": o_half[:rest],
        "d": o_half[rest:],
        "pack": pack,
    }
    far = {n: to_first(value) for n, value in far.items()}
    for n in "abcd":
        far[n + "2"] = to_sibling(far[n])

    mine = activations[:, 0]
    other = yswap(mine)
    pair = jnp.stack([jnp.where(y == 0, mine, other), jnp.where(y == 0, other, mine)], axis=1)
    normed = normalize(pair.astype(jnp.float32), norm_gain[0].astype(jnp.float32)).astype(jnp.bfloat16)
    gathered = gather_ring(normed.reshape(4, 16, -1), z, (0,), far, {4: ["a"]})
    zero = jnp.zeros((), jnp.int32)
    scalars = jnp.stack([z, zero, zero]).astype(jnp.int32)
    terms, four_a, four_b = layer_call(scalars, gathered, pack, (q, k, v, o))
    four_a = hold(four_a, far, ["b"])
    summed = scatter_ring(terms, four_a, four_b, (0,), far, {2: ["a2"], 3: ["c"], 4: ["b2", "d"]})
    summed = hold(summed.astype(jnp.bfloat16).reshape(2, 2, 16, -1), far, ["c2", "pack"])

    own = jnp.where(section == 0, summed[0], to_second(summed[1]))
    partner = yswap(own)
    stream = jnp.where(section == 0, pair[0], pair[1]).astype(jnp.float32)
    stream = (stream + (own.astype(jnp.float32) + partner.astype(jnp.float32))).astype(jnp.bfloat16)
    pack_second = jnp.where(section == 0, far["pack"], pack)
    normed = normalize(stream.astype(jnp.float32), pack_second[RANK].astype(jnp.float32)).astype(jnp.bfloat16)
    gathered = gather_ring(normed, z, (0, 1), far, {3: ["d2"]})
    scalars = jnp.stack([z, 1 - section, core]).astype(jnp.int32)
    terms = layer_call(scalars, gathered, pack_second, (q, k, v, o), [far[n] for n in ("a", "b", "c", "d", "a2", "b2", "c2", "d2")])
    summed = scatter_ring(*terms, (0, 1), far, {})
    keep = jnp.where(y == 0, summed[0], summed[1])
    give = jnp.where(y == 0, summed[1], summed[0]).astype(jnp.bfloat16)
    got = yswap(give)
    base = jnp.where(y == 0, stream[0], stream[1]).astype(jnp.float32)
    return (base + (keep + got.astype(jnp.float32))).astype(jnp.bfloat16)[None, None]


def solution(mesh):
    return jax.shard_map(
        per_device,
        mesh=mesh,
        in_specs=(
            P(None, "dp", "tensor", None),
            P("section", None),
            P("section", None, "tensor"),
            P("section", None, "tensor"),
            P("section", None, "tensor"),
            P("section", None, None),
            P("section", None, "tensor"),
            P("section", "tensor"),
            P("section", "tensor"),
            P("section", "tensor", None),
        ),
        out_specs=P("section", "dp", "tensor", None),
        check_vma=False,
    )
```

```python
import functools

import jax
import jax.numpy as jnp
from jax import lax
from jax.experimental import pallas as pl
from jax.experimental.pallas import tpu as pltpu
from jax.sharding import PartitionSpec as P

Z = 8
KEY = 64
VAL = 128
LEN = 256
RANK = 16
PACK = 40
OFFSETS = (0, 1, 2, 3, 5, 6, 7)


def zp(value):
    return lax.ppermute(value, "tensor", [(y * Z + z, y * Z + (z + 1) % Z) for y in range(2) for z in range(Z)])


def zm(value):
    return lax.ppermute(value, "tensor", [(y * Z + z, y * Z + (z + Z - 1) % Z) for y in range(2) for z in range(Z)])


def yswap(value):
    return lax.ppermute(value, "tensor", [(t, t ^ Z) for t in range(2 * Z)])


def to_second(value):
    n = 2 * Z
    return lax.ppermute(value, ("section", "tensor"), [(t, n + t) for t in range(n)])


def to_first(value):
    n = 2 * Z
    return lax.ppermute(value, ("section", "tensor"), [(n + t, t) for t in range(n)])


def to_sibling(value):
    return lax.ppermute(value, "dp", [(d, d ^ 1) for d in range(lax.axis_size("dp"))])


def normalize(values, gain):
    return values * lax.rsqrt(jnp.mean(values * values, axis=-1, keepdims=True) + 1e-05) * gain


def hold(value, far, names):
    if names:
        value, *arrived = lax.optimization_barrier((value, *[far[n] for n in names]))
        far.update(zip(names, arrived))
    return value


def gather_ring(block, z, far, at, later=0):
    groups, size, depth = block.shape
    half = groups // 2

    def place(x, block, offset, first=0):
        return lax.dynamic_update_slice(x, block, (first, (z + offset) % Z * size, 0))

    p, m = zp(block), zm(block)
    block, p, later = lax.optimization_barrier((block, p, later))
    x = jnp.tile(block, (1, Z, 1))
    for step in (2, 3):
        x = place(place(x, p, Z + 1 - step), m, step - 1)
        p, m = zp(hold(p, far, at.get(step))), zm(m)
    x = place(place(x, p, Z - 3), m, 3)
    p, m = zp(hold(p[:half], far, at.get(4))), zm(m[half:])
    return place(place(x, p, 4), m, 4, half), later


def add(a, b):
    return (a.astype(jnp.float32) + b.astype(jnp.float32)).astype(jnp.bfloat16)


def scatter_ring(terms, four_a, four_b, far, at):
    half = four_a.shape[0]
    p, m = zp(four_a), zm(four_b)
    up = jnp.concatenate([add(terms[3][:half], p), terms[3][half:]], 0)
    down = jnp.concatenate([terms[5][:half], add(terms[5][half:], m)], 0)
    p, m = zp(hold(up, far, at.get(2))), zm(down)
    p, m = zp(hold(add(terms[2], p), far, at.get(3))), zm(add(terms[6], m))
    p, m = zp(hold(add(terms[1], p), far, at.get(4))), zm(add(terms[7], m))
    return terms[0].astype(jnp.float32) + p.astype(jnp.float32) + m.astype(jnp.float32)


def nt(a, b):
    return lax.dot_general(a, b, (((1,), (1,)), ((), ())), preferred_element_type=jnp.float32)


def mix(q, k, v, low, up, bias, gain):
    width = q.shape[1]
    heads = width // KEY
    half = LEN // 2
    bf = jnp.bfloat16
    logits = jnp.dot(low, up, preferred_element_type=jnp.float32) + bias
    log_sig = jnp.minimum(logits, 0.0) - jnp.log(1.0 + jnp.exp(-jnp.abs(logits)))
    decay = jnp.exp(log_sig * (1.0 / 16.0))
    q = q.astype(jnp.float32) * KEY ** -0.5
    row = lax.broadcasted_iota(jnp.int32, (LEN, width), 0)
    lane_head = lax.broadcasted_iota(jnp.int32, (1, width), 1) // KEY
    head_masks = [jnp.where(lane_head == h, 1.0, 0.0).astype(bf) for h in range(heads)]
    i = lax.broadcasted_iota(jnp.int32, (half, half), 0)
    j = lax.broadcasted_iota(jnp.int32, (half, half), 1)
    apart = jnp.where(i > j, i ^ j, 0)
    first, second = slice(0, half), slice(half, LEN)

    def scores(qb, kb):
        lhs = jnp.concatenate([qb * m for m in head_masks], axis=0)
        return nt(lhs, kb).reshape(heads, qb.shape[0], half)

    qb = q.astype(bf)
    att = [jnp.where((i == j)[None], scores(qb[s], k[s]), 0.0) for s in (first, second)]
    q, k, total = q * decay, k.astype(jnp.float32), decay
    for level in range(3):
        b = 1 << level
        qb, kb = q.astype(bf), k.astype(bf)
        mask = ((apart >> level) == 1)[None]
        att = [jnp.where(mask, scores(qb[s], kb[s]), a) for s, a in zip((first, second), att)]
        upper = (row & b) != 0
        other = jnp.where(upper, pltpu.roll(total, b, 0), pltpu.roll(total, LEN - b, 0))
        q = jnp.where(upper, q * other, q)
        k = jnp.where(upper, k, k * other)
        total = total * other
    total = total.reshape(LEN // 8, 8, width)
    for level in range(3, 7):
        b = 1 << level
        pairs = half // (2 * b)
        kb = k.astype(bf)
        q = q.reshape(2 * pairs, 2, b, width)
        qb = q[:, 1].astype(bf).reshape(2, half // 2, width)
        mask = ((apart >> level) == 1).astype(jnp.int32).reshape(pairs, 2, b, half)[:, 1] == 1
        for n, s in enumerate((first, second)):
            a = att[n].reshape(heads, pairs, 2, b, half)
            upper = jnp.where(mask[None], scores(qb[n], kb[s]).reshape(heads, pairs, b, half), a[:, :, 1])
            att[n] = jnp.stack([a[:, :, 0], upper], axis=2).reshape(heads, half, half)
        total = total.reshape(2 * pairs, 2, 1, 8, width)
        begins, ends = total[:, 0], total[:, 1]
        upper = (q[:, 1].reshape(2 * pairs, b // 8, 8, width) * begins).reshape(2 * pairs, b, width)
        q = jnp.stack([q[:, 0], upper], axis=1).reshape(LEN, width)
        k = k.reshape(2 * pairs, 2, b, width)
        lower = (k[:, 0].reshape(2 * pairs, b // 8, 8, width) * ends).reshape(2 * pairs, b, width)
        k = jnp.stack([lower, k[:, 1]], axis=1).reshape(LEN, width)
        total = begins * ends
    across = scores(q[second].astype(bf), k[first].astype(bf))
    outs = []
    for h in range(heads):
        vh = v[:, h * VAL:(h + 1) * VAL]
        top = jnp.dot(att[0][h].astype(bf), vh[first], preferred_element_type=jnp.float32)
        bottom = jnp.dot(jnp.concatenate([across[h], att[1][h]], axis=1).astype(bf), vh,
                         preferred_element_type=jnp.float32)
        mixed = jnp.concatenate([top, bottom], axis=0)
        scale = lax.rsqrt(jnp.maximum(jnp.mean(mixed * mixed, axis=-1, keepdims=True), 1.0))
        outs.append((mixed * scale * gain[:, h * VAL:(h + 1) * VAL]).astype(bf))
    return jnp.concatenate(outs, axis=1)


def layer_kernel(groups, n_halves, scalars, *refs):
    at = 0

    def take(count):
        nonlocal at
        out = refs[at:at + count]
        at += count
        return out

    x, pack, q_src, k_src, v_src, o_src = take(6)
    halves = take(n_halves)
    outs = take(9)
    w, wo, y, gated, sem = take(5)
    half = groups // 2
    z, fetched, core = scalars[0], scalars[1], scalars[2]
    depth = x.shape[1]
    wide = w.shape[2]

    sources = [(q_src, slice(None)), (k_src, slice(None)), (v_src, slice(0, wide)), (v_src, slice(wide, 2 * wide)),
               (o_src, slice(None))]
    targets = [w.at[0], w.at[1], w.at[2], w.at[3], wo]

    def own_copy(index):
        src, columns = sources[index]
        return pltpu.make_async_copy(src.at[:, columns], targets[index], sem.at[index])

    def start_own():
        for index in range(5):
            own_copy(index).start()

    def start_halves():
        most = wide // 2
        for (a, b, c, d), side in ((halves[0:4], core), (halves[4:8], 1 - core)):
            rows = pl.ds(pl.multiple_of(side * (depth // 2), depth // 2), depth // 2)
            low_rows = pl.ds(pl.multiple_of(side * wide, wide), most)
            high_rows = pl.ds(pl.multiple_of(side * wide + most, most), most)
            for index, src, dst in (
                (0, a.at[:, 0:wide], w.at[0, rows, :]),
                (1, a.at[:, wide:2 * wide], w.at[1, rows, :]),
                (2, a.at[:, 2 * wide:], w.at[2, rows, 0:most]),
                (2, b.at[:, 0:most], w.at[2, rows, most:]),
                (3, b.at[:, most:], w.at[3, rows, :]),
                (4, c, wo.at[low_rows, :]),
                (4, d, wo.at[high_rows, :]),
            ):
                pltpu.make_async_copy(src, dst, sem.at[index]).start()

    if n_halves:
        pl.when(fetched == 0)(start_own)
        pl.when(fetched == 1)(start_halves)
    else:
        start_own()

    low = nt(x[...], pack[0:RANK, :]).astype(jnp.bfloat16)

    for index in range(4):
        own_copy(index).wait()
        y[index] = jnp.dot(x[...], w[index], preferred_element_type=jnp.float32).astype(jnp.bfloat16)
    gain = pack[17:18, 0:2 * wide].astype(jnp.float32)
    bias = sum(pack[r:r + 1, 0:wide].astype(jnp.float32) for r in (18, 19, 20))
    up = pack[24:24 + RANK, 0:wide]
    for n in range(groups // 2):
        s = slice(n * LEN, (n + 1) * LEN)
        v = jnp.concatenate([y[2, s, :], y[3, s, :]], axis=1)
        mixed = mix(y[0, s, :], y[1, s, :], v, low[s], up, bias, gain)
        for g in range(2):
            for to in range(Z):
                at = pl.multiple_of((lax.rem(to - z + Z, Z) * groups + 2 * n + g) * 16, 16)
                gated[pl.ds(at, 16), :] = mixed[g * 128 + to * 16:g * 128 + to * 16 + 16]
    own_copy(4).wait()
    step = 512
    for c in range(depth // step):
        cols = slice(c * step, (c + 1) * step)
        part = jnp.dot(gated[...], wo[:, cols], preferred_element_type=jnp.float32).astype(jnp.bfloat16)
        part = part.reshape(Z, groups, 16, step)
        for n, offset in enumerate(OFFSETS):
            outs[n][:, :, cols] = part[offset]
        outs[7][:, :, cols] = part[4, 0:half]
        outs[8][:, :, cols] = part[4, half:groups]


def layer_call(scalars, gathered, pack, weights, halves=()):
    groups, _, depth = gathered.shape
    count = groups * 128
    bf = jnp.bfloat16
    part = jax.ShapeDtypeStruct((groups // 2, 16, depth), bf)
    hbm = pl.BlockSpec(memory_space=pltpu.HBM)
    vmem = pl.BlockSpec(memory_space=pltpu.VMEM)
    wide = weights[0].shape[1]
    operands = [gathered.reshape(count, depth), pack, *weights, *halves]
    outs = pl.pallas_call(
        functools.partial(layer_kernel, groups, len(halves)),
        out_shape=[jax.ShapeDtypeStruct((groups, 16, depth), bf)] * 7 + [part] * 2,
        in_specs=[pl.BlockSpec(memory_space=pltpu.SMEM)] + [vmem] * 2 + [hbm] * (4 + len(halves)),
        out_specs=[vmem] * 9,
        scratch_shapes=[
            pltpu.VMEM((4, depth, wide), bf),
            pltpu.VMEM((2 * wide, depth), bf),
            pltpu.VMEM((4, count, wide), bf),
            pltpu.VMEM((count, 2 * wide), bf),
            pltpu.SemaphoreType.DMA((5,)),
        ],
        compiler_params=pltpu.CompilerParams(vmem_limit_bytes=50 * 1024 * 1024),
        cost_estimate=pl.CostEstimate(flops=count * depth, bytes_accessed=count * depth, transcendentals=0),
    )(scalars, *operands)
    return dict(zip(OFFSETS, outs[:7])), outs[7], outs[8]


def make_pack(norm_gain, decay_down, decay_up, decay_bias, head_gain):
    depth = norm_gain.shape[0]

    def wide(rows):
        return jnp.pad(rows.astype(jnp.bfloat16), ((0, 0), (0, depth - rows.shape[1])))

    high = lax.reduce_precision(decay_bias, 8, 7)
    middle = lax.reduce_precision(decay_bias - high, 8, 7)
    bias = jnp.stack([high, middle, decay_bias - high - middle])
    return jnp.concatenate([
        decay_down.T, norm_gain[None], wide(head_gain[None]), wide(bias),
        jnp.zeros((24 - RANK - 5, depth), jnp.bfloat16), wide(decay_up),
    ], axis=0)


def per_device(activations, norm_gain, query_matrix, key_weight, value_weight, decay_down, decay_up,
               decay_bias, head_gain, output_matrix):
    section = lax.axis_index("section")
    core = lax.axis_index("dp") % 2
    tensor = lax.axis_index("tensor")
    y, z = tensor // Z, tensor % Z
    q, k, v, o = query_matrix[0], key_weight[0], value_weight[0], output_matrix[0]

    def half_of(rows):
        return lax.dynamic_slice_in_dim(rows, core * (rows.shape[0] // 2), rows.shape[0] // 2, 0)

    most = v.shape[1] // 4
    o_half = half_of(o)
    rest = o_half.shape[0] // 2
    far = {
        "a": jnp.concatenate([half_of(q), half_of(k), half_of(v[:, :most])], axis=1),
        "b": half_of(v[:, most:]),
        "c": o_half[:rest],
        "d": o_half[rest:],
    }
    far = {n: to_first(value) for n, value in far.items()}
    for n in "abcd":
        far[n + "2"] = to_sibling(far[n])

    mine = activations[:, 0]
    other = yswap(mine)
    pair = jnp.stack([jnp.where(y == 0, mine, other), jnp.where(y == 0, other, mine)], axis=1)
    normed = normalize(pair.astype(jnp.float32), norm_gain[0].astype(jnp.float32)).astype(jnp.bfloat16)
    gathered, down = gather_ring(normed.reshape(4, 16, -1), z, far, {}, decay_down[0])
    pack = make_pack(norm_gain[0], down, decay_up[0], decay_bias[0], head_gain[0])
    far["pack"] = to_first(pack)
    zero = jnp.zeros((), jnp.int32)
    scalars = jnp.stack([z, zero, zero]).astype(jnp.int32)
    scalars = hold(scalars, far, ["a"])
    terms, four_a, four_b = layer_call(scalars, gathered, pack, (q, k, v, o))
    four_a = hold(four_a, far, ["b"])
    summed = scatter_ring(terms, four_a, four_b, far, {2: ["a2"], 3: ["c"], 4: ["b2", "d"]})
    summed = hold(summed.astype(jnp.bfloat16).reshape(2, 2, 16, -1), far, ["c2", "pack"])

    own = jnp.where(section == 0, summed[0], to_second(summed[1]))
    partner = yswap(own)
    stream = jnp.where(section == 0, pair[0], pair[1]).astype(jnp.float32)
    stream = (stream + (own.astype(jnp.float32) + partner.astype(jnp.float32))).astype(jnp.bfloat16)
    pack_second = jnp.where(section == 0, far["pack"], pack)
    normed = normalize(stream.astype(jnp.float32), pack_second[RANK].astype(jnp.float32)).astype(jnp.bfloat16)
    gathered, _ = gather_ring(normed, z, far, {3: ["d2"]})
    scalars = jnp.stack([z, 1 - section, core]).astype(jnp.int32)
    terms = layer_call(scalars, gathered, pack_second, (q, k, v, o), [far[n] for n in ("a", "b", "c", "d", "a2", "b2", "c2", "d2")])
    summed = scatter_ring(*terms, far, {})
    keep = jnp.where(y == 0, summed[0], summed[1])
    give = jnp.where(y == 0, summed[1], summed[0]).astype(jnp.bfloat16)
    got = yswap(give)
    base = jnp.where(y == 0, stream[0], stream[1]).astype(jnp.float32)
    return (base + (keep + got.astype(jnp.float32))).astype(jnp.bfloat16)[None, None]


def solution(mesh):
    return jax.shard_map(
        per_device,
        mesh=mesh,
        in_specs=(
            P(None, "dp", "tensor", None),
            P("section", None),
            P("section", None, "tensor"),
            P("section", None, "tensor"),
            P("section", None, "tensor"),
            P("section", None, None),
            P("section", None, "tensor"),
            P("section", "tensor"),
            P("section", "tensor"),
            P("section", "tensor", None),
        ),
        out_specs=P("section", "dp", "tensor", None),
        check_vma=False,
    )
```

```python
import functools

import jax
import jax.numpy as jnp
from jax import lax
from jax.experimental import pallas as pl
from jax.experimental.pallas import tpu as pltpu
from jax.sharding import PartitionSpec as P

Z = 8
KEY = 64
VAL = 128
LEN = 256
RANK = 16
PACK = 40
OFFSETS = (0, 1, 2, 3, 5, 6, 7)


def zp(value):
    return lax.ppermute(value, "tensor", [(y * Z + z, y * Z + (z + 1) % Z) for y in range(2) for z in range(Z)])


def zm(value):
    return lax.ppermute(value, "tensor", [(y * Z + z, y * Z + (z + Z - 1) % Z) for y in range(2) for z in range(Z)])


def yswap(value):
    return lax.ppermute(value, "tensor", [(t, t ^ Z) for t in range(2 * Z)])


def to_second(value):
    n = 2 * Z
    return lax.ppermute(value, ("section", "tensor"), [(t, n + t) for t in range(n)])


def to_first(value):
    n = 2 * Z
    return lax.ppermute(value, ("section", "tensor"), [(n + t, t) for t in range(n)])


def to_sibling(value):
    return lax.ppermute(value, "dp", [(d, d ^ 1) for d in range(lax.axis_size("dp"))])


def normalize(values, gain):
    return values * lax.rsqrt(jnp.mean(values * values, axis=-1, keepdims=True) + 1e-05) * gain


def hold(value, far, names):
    if names:
        value, *arrived = lax.optimization_barrier((value, *[far[n] for n in names]))
        far.update(zip(names, arrived))
    return value


def gather_ring(block, z, far, at, later=0):
    groups, size, depth = block.shape
    half = groups // 2

    def place(x, block, offset, first=0):
        return lax.dynamic_update_slice(x, block, (first, (z + offset) % Z * size, 0))

    p, m = zp(block), zm(block)
    block, p, later = lax.optimization_barrier((block, p, later))
    x = jnp.tile(block, (1, Z, 1))
    for step in (2, 3):
        x = place(place(x, p, Z + 1 - step), m, step - 1)
        p, m = zp(hold(p, far, at.get(step))), zm(m)
    x = place(place(x, p, Z - 3), m, 3)
    p, m = zp(hold(p[:half], far, at.get(4))), zm(m[half:])
    return place(place(x, p, 4), m, 4, half), later


def add(a, b):
    return (a.astype(jnp.float32) + b.astype(jnp.float32)).astype(jnp.bfloat16)


def scatter_ring(terms, four_a, four_b, far, at):
    half = four_a.shape[0]
    p, m = zp(four_a), zm(four_b)
    up = jnp.concatenate([add(terms[3][:half], p), terms[3][half:]], 0)
    down = jnp.concatenate([terms[5][:half], add(terms[5][half:], m)], 0)
    p, m = zp(hold(up, far, at.get(2))), zm(down)
    p, m = zp(hold(add(terms[2], p), far, at.get(3))), zm(add(terms[6], m))
    p, m = zp(hold(add(terms[1], p), far, at.get(4))), zm(add(terms[7], m))
    return terms[0].astype(jnp.float32) + p.astype(jnp.float32) + m.astype(jnp.float32)


def nt(a, b):
    return lax.dot_general(a, b, (((1,), (1,)), ((), ())), preferred_element_type=jnp.float32)


def mix(q, k, v, low, up, bias, gain):
    width = q.shape[1]
    heads = width // KEY
    half = LEN // 2
    bf = jnp.bfloat16
    logits = jnp.dot(low, up, preferred_element_type=jnp.float32) + bias
    log_sig = jnp.minimum(logits, 0.0) - jnp.log(1.0 + jnp.exp(-jnp.abs(logits)))
    decay = jnp.exp(log_sig * (1.0 / 16.0))
    q = q.astype(jnp.float32) * KEY ** -0.5
    row = lax.broadcasted_iota(jnp.int32, (LEN, width), 0)
    lane_head = lax.broadcasted_iota(jnp.int32, (1, width), 1) // KEY
    head_masks = [jnp.where(lane_head == h, 1.0, 0.0).astype(bf) for h in range(heads)]
    i = lax.broadcasted_iota(jnp.int32, (half, half), 0)
    j = lax.broadcasted_iota(jnp.int32, (half, half), 1)
    apart = jnp.where(i > j, i ^ j, 0)
    first, second = slice(0, half), slice(half, LEN)

    def scores(qb, kb):
        lhs = jnp.concatenate([qb * m for m in head_masks], axis=0)
        return nt(lhs, kb).reshape(heads, qb.shape[0], half)

    qb = q.astype(bf)
    att = [jnp.where((i == j)[None], scores(qb[s], k[s]), 0.0) for s in (first, second)]
    q, k, total = q * decay, k.astype(jnp.float32), decay
    for level in range(3):
        b = 1 << level
        qb, kb = q.astype(bf), k.astype(bf)
        mask = ((apart >> level) == 1)[None]
        att = [jnp.where(mask, scores(qb[s], kb[s]), a) for s, a in zip((first, second), att)]
        upper = (row & b) != 0
        other = jnp.where(upper, pltpu.roll(total, b, 0), pltpu.roll(total, LEN - b, 0))
        q = jnp.where(upper, q * other, q)
        k = jnp.where(upper, k, k * other)
        total = total * other
    total = total.reshape(LEN // 8, 8, width)
    for level in range(3, 7):
        b = 1 << level
        pairs = half // (2 * b)
        kb = k.astype(bf)
        q = q.reshape(2 * pairs, 2, b, width)
        qb = q[:, 1].astype(bf).reshape(2, half // 2, width)
        mask = ((apart >> level) == 1).astype(jnp.int32).reshape(pairs, 2, b, half)[:, 1] == 1
        for n, s in enumerate((first, second)):
            a = att[n].reshape(heads, pairs, 2, b, half)
            upper = jnp.where(mask[None], scores(qb[n], kb[s]).reshape(heads, pairs, b, half), a[:, :, 1])
            att[n] = jnp.stack([a[:, :, 0], upper], axis=2).reshape(heads, half, half)
        total = total.reshape(2 * pairs, 2, 1, 8, width)
        begins, ends = total[:, 0], total[:, 1]
        upper = (q[:, 1].reshape(2 * pairs, b // 8, 8, width) * begins).reshape(2 * pairs, b, width)
        q = jnp.stack([q[:, 0], upper], axis=1).reshape(LEN, width)
        k = k.reshape(2 * pairs, 2, b, width)
        lower = (k[:, 0].reshape(2 * pairs, b // 8, 8, width) * ends).reshape(2 * pairs, b, width)
        k = jnp.stack([lower, k[:, 1]], axis=1).reshape(LEN, width)
        total = begins * ends
    across = scores(q[second].astype(bf), k[first].astype(bf))
    outs = []
    for h in range(heads):
        vh = v[:, h * VAL:(h + 1) * VAL]
        top = jnp.dot(att[0][h].astype(bf), vh[first], preferred_element_type=jnp.float32)
        bottom = jnp.dot(jnp.concatenate([across[h], att[1][h]], axis=1).astype(bf), vh,
                         preferred_element_type=jnp.float32)
        mixed = jnp.concatenate([top, bottom], axis=0)
        scale = lax.rsqrt(jnp.maximum(jnp.mean(mixed * mixed, axis=-1, keepdims=True), 1.0))
        outs.append((mixed * scale * gain[:, h * VAL:(h + 1) * VAL]).astype(bf))
    return jnp.concatenate(outs, axis=1)


def layer_kernel(groups, n_halves, scalars, *refs):
    at = 0

    def take(count):
        nonlocal at
        out = refs[at:at + count]
        at += count
        return out

    x, pack, q_src, k_src, v_src, o_src = take(6)
    halves = take(n_halves)
    outs = take(9)
    w, wo, y, gated, sem = take(5)
    half = groups // 2
    z, fetched, core = scalars[0], scalars[1], scalars[2]
    depth = x.shape[1]
    wide = w.shape[2]

    sources = [(q_src, slice(None)), (k_src, slice(None)), (v_src, slice(0, wide)), (v_src, slice(wide, 2 * wide)),
               (o_src, slice(None))]
    targets = [w.at[0], w.at[1], w.at[2], w.at[3], wo]

    def own_copy(index):
        src, columns = sources[index]
        return pltpu.make_async_copy(src.at[:, columns], targets[index], sem.at[index])

    def start_own():
        for index in range(5):
            own_copy(index).start()

    def start_halves():
        for (a, b, c), side in ((halves[0:3], core), (halves[3:6], 1 - core)):
            rows = pl.ds(pl.multiple_of(side * (depth // 2), depth // 2), depth // 2)
            o_rows = pl.ds(pl.multiple_of(side * wide, wide), wide)
            for index, src, dst in (
                (0, a.at[:, 0:wide], w.at[0, rows, :]),
                (1, a.at[:, wide:2 * wide], w.at[1, rows, :]),
                (2, b.at[:, 0:wide], w.at[2, rows, :]),
                (3, b.at[:, wide:], w.at[3, rows, :]),
                (4, c, wo.at[o_rows, :]),
            ):
                pltpu.make_async_copy(src, dst, sem.at[index]).start()

    if n_halves:
        pl.when(fetched == 0)(start_own)
        pl.when(fetched == 1)(start_halves)
    else:
        start_own()

    low = nt(x[...], pack[0:RANK, :]).astype(jnp.bfloat16)

    for index in range(4):
        own_copy(index).wait()
        y[index] = jnp.dot(x[...], w[index], preferred_element_type=jnp.float32).astype(jnp.bfloat16)
    gain = pack[17:18, 0:2 * wide].astype(jnp.float32)
    bias = sum(pack[r:r + 1, 0:wide].astype(jnp.float32) for r in (18, 19, 20))
    up = pack[24:24 + RANK, 0:wide]
    for n in range(groups // 2):
        s = slice(n * LEN, (n + 1) * LEN)
        v = jnp.concatenate([y[2, s, :], y[3, s, :]], axis=1)
        mixed = mix(y[0, s, :], y[1, s, :], v, low[s], up, bias, gain)
        for g in range(2):
            for to in range(Z):
                at = pl.multiple_of((lax.rem(to - z + Z, Z) * groups + 2 * n + g) * 16, 16)
                gated[pl.ds(at, 16), :] = mixed[g * 128 + to * 16:g * 128 + to * 16 + 16]
    own_copy(4).wait()
    step = 512
    for c in range(depth // step):
        cols = slice(c * step, (c + 1) * step)
        part = jnp.dot(gated[...], wo[:, cols], preferred_element_type=jnp.float32).astype(jnp.bfloat16)
        part = part.reshape(Z, groups, 16, step)
        for n, offset in enumerate(OFFSETS):
            outs[n][:, :, cols] = part[offset]
        outs[7][:, :, cols] = part[4, 0:half]
        outs[8][:, :, cols] = part[4, half:groups]


def layer_call(scalars, gathered, pack, weights, halves=()):
    groups, _, depth = gathered.shape
    count = groups * 128
    bf = jnp.bfloat16
    part = jax.ShapeDtypeStruct((groups // 2, 16, depth), bf)
    hbm = pl.BlockSpec(memory_space=pltpu.HBM)
    vmem = pl.BlockSpec(memory_space=pltpu.VMEM)
    wide = weights[0].shape[1]
    operands = [gathered.reshape(count, depth), pack, *weights, *halves]
    outs = pl.pallas_call(
        functools.partial(layer_kernel, groups, len(halves)),
        out_shape=[jax.ShapeDtypeStruct((groups, 16, depth), bf)] * 7 + [part] * 2,
        in_specs=[pl.BlockSpec(memory_space=pltpu.SMEM)] + [vmem] * 2 + [hbm] * (4 + len(halves)),
        out_specs=[vmem] * 9,
        scratch_shapes=[
            pltpu.VMEM((4, depth, wide), bf),
            pltpu.VMEM((2 * wide, depth), bf),
            pltpu.VMEM((4, count, wide), bf),
            pltpu.VMEM((count, 2 * wide), bf),
            pltpu.SemaphoreType.DMA((5,)),
        ],
        compiler_params=pltpu.CompilerParams(vmem_limit_bytes=50 * 1024 * 1024),
        cost_estimate=pl.CostEstimate(flops=count * depth, bytes_accessed=count * depth, transcendentals=0),
    )(scalars, *operands)
    return dict(zip(OFFSETS, outs[:7])), outs[7], outs[8]


def make_pack(norm_gain, decay_down, decay_up, decay_bias, head_gain):
    depth = norm_gain.shape[0]

    def wide(rows):
        return jnp.pad(rows.astype(jnp.bfloat16), ((0, 0), (0, depth - rows.shape[1])))

    high = lax.reduce_precision(decay_bias, 8, 7)
    middle = lax.reduce_precision(decay_bias - high, 8, 7)
    bias = jnp.stack([high, middle, decay_bias - high - middle])
    return jnp.concatenate([
        decay_down.T, norm_gain[None], wide(head_gain[None]), wide(bias),
        jnp.zeros((24 - RANK - 5, depth), jnp.bfloat16), wide(decay_up),
    ], axis=0)


def per_device(activations, norm_gain, query_matrix, key_weight, value_weight, decay_down, decay_up,
               decay_bias, head_gain, output_matrix):
    section = lax.axis_index("section")
    core = lax.axis_index("dp") % 2
    tensor = lax.axis_index("tensor")
    y, z = tensor // Z, tensor % Z
    q, k, v, o = query_matrix[0], key_weight[0], value_weight[0], output_matrix[0]

    def half_of(rows):
        return lax.dynamic_slice_in_dim(rows, core * (rows.shape[0] // 2), rows.shape[0] // 2, 0)

    far = {
        "a": jnp.concatenate([half_of(q), half_of(k)], axis=1),
        "b": half_of(v),
        "c": half_of(o),
    }
    far = {n: to_first(value) for n, value in far.items()}
    for n in "abc":
        far[n + "2"] = to_sibling(far[n])

    mine = activations[:, 0]
    other = yswap(mine)
    pair = jnp.stack([jnp.where(y == 0, mine, other), jnp.where(y == 0, other, mine)], axis=1)
    normed = normalize(pair.astype(jnp.float32), norm_gain[0].astype(jnp.float32)).astype(jnp.bfloat16)
    gathered, down = gather_ring(normed.reshape(4, 16, -1), z, far, {}, decay_down[0])
    pack = make_pack(norm_gain[0], down, decay_up[0], decay_bias[0], head_gain[0])
    far["pack"] = to_first(pack)
    zero = jnp.zeros((), jnp.int32)
    scalars = jnp.stack([z, zero, zero]).astype(jnp.int32)
    scalars = hold(scalars, far, ["a"])
    terms, four_a, four_b = layer_call(scalars, gathered, pack, (q, k, v, o))
    summed = scatter_ring(terms, four_a, four_b, far, {2: ["a2"], 3: ["b"]})
    summed = hold(summed.astype(jnp.bfloat16).reshape(2, 2, 16, -1), far, ["b2", "pack"])

    own = jnp.where(section == 0, summed[0], to_second(summed[1]))
    own = hold(own, far, ["c"])
    partner = yswap(own)
    stream = jnp.where(section == 0, pair[0], pair[1]).astype(jnp.float32)
    stream = (stream + (own.astype(jnp.float32) + partner.astype(jnp.float32))).astype(jnp.bfloat16)
    pack_second = jnp.where(section == 0, far["pack"], pack)
    normed = normalize(stream.astype(jnp.float32), pack_second[RANK].astype(jnp.float32)).astype(jnp.bfloat16)
    gathered, _ = gather_ring(normed, z, far, {4: ["c2"]})
    scalars = jnp.stack([z, 1 - section, core]).astype(jnp.int32)
    terms = layer_call(scalars, gathered, pack_second, (q, k, v, o), [far[n] for n in ("a", "b", "c", "a2", "b2", "c2")])
    summed = scatter_ring(*terms, far, {})
    keep = jnp.where(y == 0, summed[0], summed[1])
    give = jnp.where(y == 0, summed[1], summed[0]).astype(jnp.bfloat16)
    got = yswap(give)
    base = jnp.where(y == 0, stream[0], stream[1]).astype(jnp.float32)
    return (base + (keep + got.astype(jnp.float32))).astype(jnp.bfloat16)[None, None]


def solution(mesh):
    return jax.shard_map(
        per_device,
        mesh=mesh,
        in_specs=(
            P(None, "dp", "tensor", None),
            P("section", None),
            P("section", None, "tensor"),
            P("section", None, "tensor"),
            P("section", None, "tensor"),
            P("section", None, None),
            P("section", None, "tensor"),
            P("section", "tensor"),
            P("section", "tensor"),
            P("section", "tensor", None),
        ),
        out_specs=P("section", "dp", "tensor", None),
        check_vma=False,
    )
```

```python
import functools

import jax
import jax.numpy as jnp
from jax import lax
from jax.experimental import pallas as pl
from jax.experimental.pallas import tpu as pltpu
from jax.sharding import PartitionSpec as P

Z = 8
KEY = 64
VAL = 128
LEN = 256
RANK = 16
PACK = 40
OFFSETS = (0, 1, 2, 3, 5, 6, 7)


def zp(value):
    return lax.ppermute(value, "tensor", [(y * Z + z, y * Z + (z + 1) % Z) for y in range(2) for z in range(Z)])


def zm(value):
    return lax.ppermute(value, "tensor", [(y * Z + z, y * Z + (z + Z - 1) % Z) for y in range(2) for z in range(Z)])


def yswap(value):
    return lax.ppermute(value, "tensor", [(t, t ^ Z) for t in range(2 * Z)])


def to_second(value):
    n = 2 * Z
    return lax.ppermute(value, ("section", "tensor"), [(t, n + (t ^ Z)) for t in range(n)])


def to_first(value):
    n = 2 * Z
    return lax.ppermute(value, ("section", "tensor"), [(n + t, t ^ Z) for t in range(n)])


def to_sibling(value):
    return lax.ppermute(value, "dp", [(d, d ^ 1) for d in range(lax.axis_size("dp"))])


def normalize(values, gain):
    return values * lax.rsqrt(jnp.mean(values * values, axis=-1, keepdims=True) + 1e-05) * gain


def hold(value, far, names):
    if names:
        value, *arrived = lax.optimization_barrier((value, *[far[n] for n in names]))
        far.update(zip(names, arrived))
    return value


def gather_ring(block, z, far, at, later=0):
    groups, size, depth = block.shape
    half = groups // 2

    def place(x, block, offset, first=0):
        return lax.dynamic_update_slice(x, block, (first, (z + offset) % Z * size, 0))

    p, m = zp(block), zm(block)
    block, p, later = lax.optimization_barrier((block, p, later))
    x = jnp.tile(block, (1, Z, 1))
    for step in (2, 3):
        x = place(place(x, p, Z + 1 - step), m, step - 1)
        p, m = zp(hold(p, far, at.get(step))), zm(m)
    x = place(place(x, p, Z - 3), m, 3)
    p, m = zp(hold(p[:half], far, at.get(4))), zm(m[half:])
    return place(place(x, p, 4), m, 4, half), later


def add(a, b):
    return (a.astype(jnp.float32) + b.astype(jnp.float32)).astype(jnp.bfloat16)


def scatter_ring(terms, four_a, four_b, far, at):
    half = four_a.shape[0]
    p, m = zp(four_a), zm(four_b)
    up = jnp.concatenate([add(terms[3][:half], p), terms[3][half:]], 0)
    down = jnp.concatenate([terms[5][:half], add(terms[5][half:], m)], 0)
    p, m = zp(hold(up, far, at.get(2))), zm(down)
    p, m = zp(hold(add(terms[2], p), far, at.get(3))), zm(add(terms[6], m))
    p, m = zp(hold(add(terms[1], p), far, at.get(4))), zm(add(terms[7], m))
    return terms[0].astype(jnp.float32) + p.astype(jnp.float32) + m.astype(jnp.float32)


def nt(a, b):
    return lax.dot_general(a, b, (((1,), (1,)), ((), ())), preferred_element_type=jnp.float32)


def mix(q, k, v, low, up, bias, gain):
    width = q.shape[1]
    heads = width // KEY
    half = LEN // 2
    bf = jnp.bfloat16
    logits = jnp.dot(low, up, preferred_element_type=jnp.float32) + bias
    log_sig = jnp.minimum(logits, 0.0) - jnp.log(1.0 + jnp.exp(-jnp.abs(logits)))
    decay = jnp.exp(log_sig * (1.0 / 16.0))
    q = q.astype(jnp.float32) * KEY ** -0.5
    row = lax.broadcasted_iota(jnp.int32, (LEN, width), 0)
    lane_head = lax.broadcasted_iota(jnp.int32, (1, width), 1) // KEY
    head_masks = [jnp.where(lane_head == h, 1.0, 0.0).astype(bf) for h in range(heads)]
    i = lax.broadcasted_iota(jnp.int32, (half, half), 0)
    j = lax.broadcasted_iota(jnp.int32, (half, half), 1)
    apart = jnp.where(i > j, i ^ j, 0)
    first, second = slice(0, half), slice(half, LEN)

    def scores(qb, kb):
        lhs = jnp.concatenate([qb * m for m in head_masks], axis=0)
        return nt(lhs, kb).reshape(heads, qb.shape[0], half)

    qb = q.astype(bf)
    att = [jnp.where((i == j)[None], scores(qb[s], k[s]), 0.0) for s in (first, second)]
    q, k, total = q * decay, k.astype(jnp.float32), decay
    for level in range(3):
        b = 1 << level
        qb, kb = q.astype(bf), k.astype(bf)
        mask = ((apart >> level) == 1)[None]
        att = [jnp.where(mask, scores(qb[s], kb[s]), a) for s, a in zip((first, second), att)]
        upper = (row & b) != 0
        other = jnp.where(upper, pltpu.roll(total, b, 0), pltpu.roll(total, LEN - b, 0))
        q = jnp.where(upper, q * other, q)
        k = jnp.where(upper, k, k * other)
        total = total * other
    total = total.reshape(LEN // 8, 8, width)
    for level in range(3, 7):
        b = 1 << level
        pairs = half // (2 * b)
        kb = k.astype(bf)
        q = q.reshape(2 * pairs, 2, b, width)
        qb = q[:, 1].astype(bf).reshape(2, half // 2, width)
        mask = ((apart >> level) == 1).astype(jnp.int32).reshape(pairs, 2, b, half)[:, 1] == 1
        for n, s in enumerate((first, second)):
            a = att[n].reshape(heads, pairs, 2, b, half)
            upper = jnp.where(mask[None], scores(qb[n], kb[s]).reshape(heads, pairs, b, half), a[:, :, 1])
            att[n] = jnp.stack([a[:, :, 0], upper], axis=2).reshape(heads, half, half)
        total = total.reshape(2 * pairs, 2, 1, 8, width)
        begins, ends = total[:, 0], total[:, 1]
        upper = (q[:, 1].reshape(2 * pairs, b // 8, 8, width) * begins).reshape(2 * pairs, b, width)
        q = jnp.stack([q[:, 0], upper], axis=1).reshape(LEN, width)
        k = k.reshape(2 * pairs, 2, b, width)
        lower = (k[:, 0].reshape(2 * pairs, b // 8, 8, width) * ends).reshape(2 * pairs, b, width)
        k = jnp.stack([lower, k[:, 1]], axis=1).reshape(LEN, width)
        total = begins * ends
    across = scores(q[second].astype(bf), k[first].astype(bf))
    outs = []
    for h in range(heads):
        vh = v[:, h * VAL:(h + 1) * VAL]
        top = jnp.dot(att[0][h].astype(bf), vh[first], preferred_element_type=jnp.float32)
        bottom = jnp.dot(jnp.concatenate([across[h], att[1][h]], axis=1).astype(bf), vh,
                         preferred_element_type=jnp.float32)
        mixed = jnp.concatenate([top, bottom], axis=0)
        scale = lax.rsqrt(jnp.maximum(jnp.mean(mixed * mixed, axis=-1, keepdims=True), 1.0))
        outs.append((mixed * scale * gain[:, h * VAL:(h + 1) * VAL]).astype(bf))
    return jnp.concatenate(outs, axis=1)


def layer_kernel(groups, n_halves, scalars, *refs):
    at = 0

    def take(count):
        nonlocal at
        out = refs[at:at + count]
        at += count
        return out

    x, pack, q_src, k_src, v_src, o_src = take(6)
    halves = take(n_halves)
    outs = take(9)
    w, wo, y, gated, sem = take(5)
    half = groups // 2
    z, fetched, core = scalars[0], scalars[1], scalars[2]
    depth = x.shape[1]
    wide = w.shape[2]

    sources = [(q_src, slice(None)), (k_src, slice(None)), (v_src, slice(0, wide)), (v_src, slice(wide, 2 * wide)),
               (o_src, slice(None))]
    targets = [w.at[0], w.at[1], w.at[2], w.at[3], wo]

    def own_copy(index):
        src, columns = sources[index]
        return pltpu.make_async_copy(src.at[:, columns], targets[index], sem.at[index])

    def start_own():
        for index in range(5):
            own_copy(index).start()

    def start_halves():
        for (a, b, c, d), side in ((halves[0:4], core), (halves[4:8], 1 - core)):
            rows = pl.ds(pl.multiple_of(side * (depth // 2), depth // 2), depth // 2)
            rest = c.shape[0]
            c_rows = pl.ds(pl.multiple_of(side * wide, wide), rest)
            d_rows = pl.ds(pl.multiple_of(side * wide + rest, 32), wide - rest)
            for index, src, dst in (
                (0, a.at[:, 0:wide], w.at[0, rows, :]),
                (1, a.at[:, wide:2 * wide], w.at[1, rows, :]),
                (2, b.at[:, 0:wide], w.at[2, rows, :]),
                (3, b.at[:, wide:], w.at[3, rows, :]),
                (4, c, wo.at[c_rows, :]),
                (4, d, wo.at[d_rows, :]),
            ):
                pltpu.make_async_copy(src, dst, sem.at[index]).start()

    if n_halves:
        pl.when(fetched == 0)(start_own)
        pl.when(fetched == 1)(start_halves)
    else:
        start_own()

    low = nt(x[...], pack[0:RANK, :]).astype(jnp.bfloat16)

    for index in range(4):
        own_copy(index).wait()
        y[index] = jnp.dot(x[...], w[index], preferred_element_type=jnp.float32).astype(jnp.bfloat16)
    gain = pack[17:18, 0:2 * wide].astype(jnp.float32)
    bias = sum(pack[r:r + 1, 0:wide].astype(jnp.float32) for r in (18, 19, 20))
    up = pack[24:24 + RANK, 0:wide]
    for n in range(groups // 2):
        s = slice(n * LEN, (n + 1) * LEN)
        v = jnp.concatenate([y[2, s, :], y[3, s, :]], axis=1)
        mixed = mix(y[0, s, :], y[1, s, :], v, low[s], up, bias, gain)
        for g in range(2):
            for to in range(Z):
                at = pl.multiple_of((lax.rem(to - z + Z, Z) * groups + 2 * n + g) * 16, 16)
                gated[pl.ds(at, 16), :] = mixed[g * 128 + to * 16:g * 128 + to * 16 + 16]
    own_copy(4).wait()
    step = 512
    for c in range(depth // step):
        cols = slice(c * step, (c + 1) * step)
        part = jnp.dot(gated[...], wo[:, cols], preferred_element_type=jnp.float32).astype(jnp.bfloat16)
        part = part.reshape(Z, groups, 16, step)
        for n, offset in enumerate(OFFSETS):
            outs[n][:, :, cols] = part[offset]
        outs[7][:, :, cols] = part[4, 0:half]
        outs[8][:, :, cols] = part[4, half:groups]


def layer_call(scalars, gathered, pack, weights, halves=()):
    groups, _, depth = gathered.shape
    count = groups * 128
    bf = jnp.bfloat16
    part = jax.ShapeDtypeStruct((groups // 2, 16, depth), bf)
    hbm = pl.BlockSpec(memory_space=pltpu.HBM)
    vmem = pl.BlockSpec(memory_space=pltpu.VMEM)
    wide = weights[0].shape[1]
    operands = [gathered.reshape(count, depth), pack, *weights, *halves]
    outs = pl.pallas_call(
        functools.partial(layer_kernel, groups, len(halves)),
        out_shape=[jax.ShapeDtypeStruct((groups, 16, depth), bf)] * 7 + [part] * 2,
        in_specs=[pl.BlockSpec(memory_space=pltpu.SMEM)] + [vmem] * 2 + [hbm] * (4 + len(halves)),
        out_specs=[vmem] * 9,
        scratch_shapes=[
            pltpu.VMEM((4, depth, wide), bf),
            pltpu.VMEM((2 * wide, depth), bf),
            pltpu.VMEM((4, count, wide), bf),
            pltpu.VMEM((count, 2 * wide), bf),
            pltpu.SemaphoreType.DMA((5,)),
        ],
        compiler_params=pltpu.CompilerParams(vmem_limit_bytes=50 * 1024 * 1024),
        cost_estimate=pl.CostEstimate(flops=count * depth, bytes_accessed=count * depth, transcendentals=0),
    )(scalars, *operands)
    return dict(zip(OFFSETS, outs[:7])), outs[7], outs[8]


def make_pack(norm_gain, decay_down, decay_up, decay_bias, head_gain):
    depth = norm_gain.shape[0]

    def wide(rows):
        return jnp.pad(rows.astype(jnp.bfloat16), ((0, 0), (0, depth - rows.shape[1])))

    high = lax.reduce_precision(decay_bias, 8, 7)
    middle = lax.reduce_precision(decay_bias - high, 8, 7)
    bias = jnp.stack([high, middle, decay_bias - high - middle])
    return jnp.concatenate([
        decay_down.T, norm_gain[None], wide(head_gain[None]), wide(bias),
        jnp.zeros((24 - RANK - 5, depth), jnp.bfloat16), wide(decay_up),
    ], axis=0)


def per_device(activations, norm_gain, query_matrix, key_weight, value_weight, decay_down, decay_up,
               decay_bias, head_gain, output_matrix):
    section = lax.axis_index("section")
    core = lax.axis_index("dp") % 2
    tensor = lax.axis_index("tensor")
    y, z = tensor // Z, tensor % Z
    q, k, v, o = query_matrix[0], key_weight[0], value_weight[0], output_matrix[0]

    def half_of(rows):
        return lax.dynamic_slice_in_dim(rows, core * (rows.shape[0] // 2), rows.shape[0] // 2, 0)

    o_half = half_of(o)
    rest = o_half.shape[0] * 5 // 8
    far = {
        "a": jnp.concatenate([half_of(q), half_of(k)], axis=1),
        "b": half_of(v),
        "c": o_half[:rest],
        "d": o_half[rest:],
    }
    far = {n: to_first(value) for n, value in far.items()}
    for n in "abcd":
        far[n + "2"] = to_sibling(far[n])

    mine = activations[:, 0]
    other = yswap(mine)
    pair = jnp.stack([jnp.where(y == 0, mine, other), jnp.where(y == 0, other, mine)], axis=1)
    normed = normalize(pair.astype(jnp.float32), norm_gain[0].astype(jnp.float32)).astype(jnp.bfloat16)
    gathered, down = gather_ring(normed.reshape(4, 16, -1), z, far, {}, decay_down[0])
    pack = make_pack(norm_gain[0], down, decay_up[0], decay_bias[0], head_gain[0])
    far["pack"] = to_first(pack)
    zero = jnp.zeros((), jnp.int32)
    scalars = jnp.stack([z, zero, zero]).astype(jnp.int32)
    scalars = hold(scalars, far, ["a"])
    terms, four_a, four_b = layer_call(scalars, gathered, pack, (q, k, v, o))
    summed = scatter_ring(terms, four_a, four_b, far, {2: ["a2"], 3: ["b"], 4: ["c"]})
    summed = hold(summed.astype(jnp.bfloat16).reshape(2, 2, 16, -1), far, ["b2", "d", "pack"])

    own = jnp.where(section == 0, summed[0], to_second(summed[1]))
    partner = yswap(own)
    stream = jnp.where(section == 0, pair[0], pair[1]).astype(jnp.float32)
    stream = (stream + (own.astype(jnp.float32) + partner.astype(jnp.float32))).astype(jnp.bfloat16)
    pack_second = jnp.where(section == 0, far["pack"], pack)
    normed = normalize(stream.astype(jnp.float32), pack_second[RANK].astype(jnp.float32)).astype(jnp.bfloat16)
    gathered, _ = gather_ring(normed, z, far, {2: ["c2"], 4: ["d2"]})
    scalars = jnp.stack([z, 1 - section, core]).astype(jnp.int32)
    terms = layer_call(scalars, gathered, pack_second, (q, k, v, o), [far[n] for n in ("a", "b", "c", "d", "a2", "b2", "c2", "d2")])
    summed = scatter_ring(*terms, far, {})
    keep = jnp.where(y == 0, summed[0], summed[1])
    give = jnp.where(y == 0, summed[1], summed[0]).astype(jnp.bfloat16)
    got = yswap(give)
    base = jnp.where(y == 0, stream[0], stream[1]).astype(jnp.float32)
    return (base + (keep + got.astype(jnp.float32))).astype(jnp.bfloat16)[None, None]


def solution(mesh):
    return jax.shard_map(
        per_device,
        mesh=mesh,
        in_specs=(
            P(None, "dp", "tensor", None),
            P("section", None),
            P("section", None, "tensor"),
            P("section", None, "tensor"),
            P("section", None, "tensor"),
            P("section", None, None),
            P("section", None, "tensor"),
            P("section", "tensor"),
            P("section", "tensor"),
            P("section", "tensor", None),
        ),
        out_specs=P("section", "dp", "tensor", None),
        check_vma=False,
    )
```

```python
import functools

import jax
import jax.numpy as jnp
from jax import lax
from jax.experimental import pallas as pl
from jax.experimental.pallas import tpu as pltpu
from jax.sharding import PartitionSpec as P

Z = 8
KEY = 64
VAL = 128
LEN = 256
RANK = 16
PACK = 40
OFFSETS = (0, 1, 2, 3, 5, 6, 7)


def zp(value):
    return lax.ppermute(value, "tensor", [(y * Z + z, y * Z + (z + 1) % Z) for y in range(2) for z in range(Z)])


def zm(value):
    return lax.ppermute(value, "tensor", [(y * Z + z, y * Z + (z + Z - 1) % Z) for y in range(2) for z in range(Z)])


def yswap(value):
    return lax.ppermute(value, "tensor", [(t, t ^ Z) for t in range(2 * Z)])


def to_second(value):
    n = 2 * Z
    return lax.ppermute(value, ("section", "tensor"), [(t, n + (t ^ Z)) for t in range(n)])


def to_first(value):
    n = 2 * Z
    return lax.ppermute(value, ("section", "tensor"), [(n + t, t ^ Z) for t in range(n)])


def to_sibling(value):
    return lax.ppermute(value, "dp", [(d, d ^ 1) for d in range(lax.axis_size("dp"))])


def normalize(values, gain):
    return values * lax.rsqrt(jnp.mean(values * values, axis=-1, keepdims=True) + 1e-05) * gain


def hold(value, far, names):
    if names:
        value, *arrived = lax.optimization_barrier((value, *[far[n] for n in names]))
        far.update(zip(names, arrived))
    return value


def gather_ring(block, z, far, at, later=0):
    groups, size, depth = block.shape
    half = groups // 2

    def place(x, block, offset, first=0):
        return lax.dynamic_update_slice(x, block, (first, (z + offset) % Z * size, 0))

    p, m = zp(block), zm(block)
    block, p, later = lax.optimization_barrier((block, p, later))
    x = jnp.tile(block, (1, Z, 1))
    for step in (2, 3):
        x = place(place(x, p, Z + 1 - step), m, step - 1)
        p, m = zp(hold(p, far, at.get(step))), zm(m)
    x = place(place(x, p, Z - 3), m, 3)
    p, m = zp(hold(p[:half], far, at.get(4))), zm(m[half:])
    return place(place(x, p, 4), m, 4, half), later


def add(a, b):
    return (a.astype(jnp.float32) + b.astype(jnp.float32)).astype(jnp.bfloat16)


def scatter_ring(terms, four_a, four_b, far, at):
    half = four_a.shape[0]
    p, m = zp(four_a), zm(four_b)
    up = jnp.concatenate([add(terms[3][:half], p), terms[3][half:]], 0)
    down = jnp.concatenate([terms[5][:half], add(terms[5][half:], m)], 0)
    p, m = zp(hold(up, far, at.get(2))), zm(down)
    p, m = zp(hold(add(terms[2], p), far, at.get(3))), zm(add(terms[6], m))
    p, m = zp(hold(add(terms[1], p), far, at.get(4))), zm(add(terms[7], m))
    return terms[0].astype(jnp.float32) + p.astype(jnp.float32) + m.astype(jnp.float32)


def nt(a, b):
    return lax.dot_general(a, b, (((1,), (1,)), ((), ())), preferred_element_type=jnp.float32)


def mix(q, k, v, low, up, bias, gain):
    width = q.shape[1]
    heads = width // KEY
    half = LEN // 2
    bf = jnp.bfloat16
    logits = jnp.dot(low, up, preferred_element_type=jnp.float32) + bias
    log_sig = jnp.minimum(logits, 0.0) - jnp.log(1.0 + jnp.exp(-jnp.abs(logits)))
    decay = jnp.exp(log_sig * (1.0 / 16.0))
    q = q.astype(jnp.float32) * KEY ** -0.5
    row = lax.broadcasted_iota(jnp.int32, (LEN, width), 0)
    lane_head = lax.broadcasted_iota(jnp.int32, (1, width), 1) // KEY
    head_masks = [jnp.where(lane_head == h, 1.0, 0.0).astype(bf) for h in range(heads)]
    i = lax.broadcasted_iota(jnp.int32, (half, half), 0)
    j = lax.broadcasted_iota(jnp.int32, (half, half), 1)
    apart = jnp.where(i > j, i ^ j, 0)
    first, second = slice(0, half), slice(half, LEN)

    def scores(qb, kb):
        lhs = jnp.concatenate([qb * m for m in head_masks], axis=0)
        return nt(lhs, kb).reshape(heads, qb.shape[0], half)

    qb = q.astype(bf)
    att = [jnp.where((i == j)[None], scores(qb[s], k[s]), 0.0) for s in (first, second)]
    q, k, total = q * decay, k.astype(jnp.float32), decay
    for level in range(3):
        b = 1 << level
        qb, kb = q.astype(bf), k.astype(bf)
        mask = ((apart >> level) == 1)[None]
        att = [jnp.where(mask, scores(qb[s], kb[s]), a) for s, a in zip((first, second), att)]
        upper = (row & b) != 0
        other = jnp.where(upper, pltpu.roll(total, b, 0), pltpu.roll(total, LEN - b, 0))
        q = jnp.where(upper, q * other, q)
        k = jnp.where(upper, k, k * other)
        total = total * other
    total = total.reshape(LEN // 8, 8, width)
    for level in range(3, 7):
        b = 1 << level
        pairs = half // (2 * b)
        kb = k.astype(bf)
        q = q.reshape(2 * pairs, 2, b, width)
        qb = q[:, 1].astype(bf).reshape(2, half // 2, width)
        mask = ((apart >> level) == 1).astype(jnp.int32).reshape(pairs, 2, b, half)[:, 1] == 1
        for n, s in enumerate((first, second)):
            a = att[n].reshape(heads, pairs, 2, b, half)
            upper = jnp.where(mask[None], scores(qb[n], kb[s]).reshape(heads, pairs, b, half), a[:, :, 1])
            att[n] = jnp.stack([a[:, :, 0], upper], axis=2).reshape(heads, half, half)
        total = total.reshape(2 * pairs, 2, 1, 8, width)
        begins, ends = total[:, 0], total[:, 1]
        upper = (q[:, 1].reshape(2 * pairs, b // 8, 8, width) * begins).reshape(2 * pairs, b, width)
        q = jnp.stack([q[:, 0], upper], axis=1).reshape(LEN, width)
        k = k.reshape(2 * pairs, 2, b, width)
        lower = (k[:, 0].reshape(2 * pairs, b // 8, 8, width) * ends).reshape(2 * pairs, b, width)
        k = jnp.stack([lower, k[:, 1]], axis=1).reshape(LEN, width)
        total = begins * ends
    across = scores(q[second].astype(bf), k[first].astype(bf))
    outs = []
    for h in range(heads):
        vh = v[:, h * VAL:(h + 1) * VAL]
        top = jnp.dot(att[0][h].astype(bf), vh[first], preferred_element_type=jnp.float32)
        bottom = jnp.dot(jnp.concatenate([across[h], att[1][h]], axis=1).astype(bf), vh,
                         preferred_element_type=jnp.float32)
        mixed = jnp.concatenate([top, bottom], axis=0)
        scale = lax.rsqrt(jnp.maximum(jnp.mean(mixed * mixed, axis=-1, keepdims=True), 1.0))
        outs.append((mixed * scale * gain[:, h * VAL:(h + 1) * VAL]).astype(bf))
    return jnp.concatenate(outs, axis=1)


def layer_kernel(groups, n_halves, scalars, *refs):
    at = 0

    def take(count):
        nonlocal at
        out = refs[at:at + count]
        at += count
        return out

    x, pack, q_src, k_src, v_src, o_src = take(6)
    halves = take(n_halves)
    outs = take(9)
    w, wo, y, gated, sem = take(5)
    half = groups // 2
    z, fetched, core = scalars[0], scalars[1], scalars[2]
    depth = x.shape[1]
    wide = w.shape[2]

    sources = [(q_src, slice(None)), (k_src, slice(None)), (v_src, slice(0, wide)), (v_src, slice(wide, 2 * wide)),
               (o_src, slice(None))]
    targets = [w.at[0], w.at[1], w.at[2], w.at[3], wo]

    def own_copy(index):
        src, columns = sources[index]
        return pltpu.make_async_copy(src.at[:, columns], targets[index], sem.at[index])

    def start_halves(index):
        for (a, b, c, d), side in ((halves[0:4], core), (halves[4:8], 1 - core)):
            rows = pl.ds(pl.multiple_of(side * (depth // 2), depth // 2), depth // 2)
            rest = c.shape[0]
            c_rows = pl.ds(pl.multiple_of(side * wide, wide), rest)
            d_rows = pl.ds(pl.multiple_of(side * wide + rest, 32), wide - rest)
            copies = (
                ((a.at[:, 0:wide], w.at[0, rows, :]),),
                ((a.at[:, wide:2 * wide], w.at[1, rows, :]),),
                ((b.at[:, 0:wide], w.at[2, rows, :]),),
                ((b.at[:, wide:], w.at[3, rows, :]),),
                ((c, wo.at[c_rows, :]), (d, wo.at[d_rows, :])),
            )
            for src, dst in copies[index]:
                pltpu.make_async_copy(src, dst, sem.at[index]).start()

    def start(index):
        if n_halves:
            pl.when(fetched == 0)(own_copy(index).start)
            pl.when(fetched == 1)(functools.partial(start_halves, index))
        else:
            own_copy(index).start()

    start(0)
    start(1)
    low = nt(x[...], pack[0:RANK, :]).astype(jnp.bfloat16)

    for index in range(4):
        own_copy(index).wait()
        if index < 3:
            start(index + 2)
        y[index] = jnp.dot(x[...], w[index], preferred_element_type=jnp.float32).astype(jnp.bfloat16)
    gain = pack[17:18, 0:2 * wide].astype(jnp.float32)
    bias = sum(pack[r:r + 1, 0:wide].astype(jnp.float32) for r in (18, 19, 20))
    up = pack[24:24 + RANK, 0:wide]
    for n in range(groups // 2):
        s = slice(n * LEN, (n + 1) * LEN)
        v = jnp.concatenate([y[2, s, :], y[3, s, :]], axis=1)
        mixed = mix(y[0, s, :], y[1, s, :], v, low[s], up, bias, gain)
        for g in range(2):
            for to in range(Z):
                at = pl.multiple_of((lax.rem(to - z + Z, Z) * groups + 2 * n + g) * 16, 16)
                gated[pl.ds(at, 16), :] = mixed[g * 128 + to * 16:g * 128 + to * 16 + 16]
    own_copy(4).wait()
    step = 512
    for c in range(depth // step):
        cols = slice(c * step, (c + 1) * step)
        part = jnp.dot(gated[...], wo[:, cols], preferred_element_type=jnp.float32).astype(jnp.bfloat16)
        part = part.reshape(Z, groups, 16, step)
        for n, offset in enumerate(OFFSETS):
            outs[n][:, :, cols] = part[offset]
        outs[7][:, :, cols] = part[4, 0:half]
        outs[8][:, :, cols] = part[4, half:groups]


def layer_call(scalars, gathered, pack, weights, halves=()):
    groups, _, depth = gathered.shape
    count = groups * 128
    bf = jnp.bfloat16
    part = jax.ShapeDtypeStruct((groups // 2, 16, depth), bf)
    hbm = pl.BlockSpec(memory_space=pltpu.HBM)
    vmem = pl.BlockSpec(memory_space=pltpu.VMEM)
    wide = weights[0].shape[1]
    operands = [gathered.reshape(count, depth), pack, *weights, *halves]
    outs = pl.pallas_call(
        functools.partial(layer_kernel, groups, len(halves)),
        out_shape=[jax.ShapeDtypeStruct((groups, 16, depth), bf)] * 7 + [part] * 2,
        in_specs=[pl.BlockSpec(memory_space=pltpu.SMEM)] + [vmem] * 2 + [hbm] * (4 + len(halves)),
        out_specs=[vmem] * 9,
        scratch_shapes=[
            pltpu.VMEM((4, depth, wide), bf),
            pltpu.VMEM((2 * wide, depth), bf),
            pltpu.VMEM((4, count, wide), bf),
            pltpu.VMEM((count, 2 * wide), bf),
            pltpu.SemaphoreType.DMA((5,)),
        ],
        compiler_params=pltpu.CompilerParams(vmem_limit_bytes=50 * 1024 * 1024),
        cost_estimate=pl.CostEstimate(flops=count * depth, bytes_accessed=count * depth, transcendentals=0),
    )(scalars, *operands)
    return dict(zip(OFFSETS, outs[:7])), outs[7], outs[8]


def make_pack(norm_gain, decay_down, decay_up, decay_bias, head_gain):
    depth = norm_gain.shape[0]

    def wide(rows):
        return jnp.pad(rows.astype(jnp.bfloat16), ((0, 0), (0, depth - rows.shape[1])))

    high = lax.reduce_precision(decay_bias, 8, 7)
    middle = lax.reduce_precision(decay_bias - high, 8, 7)
    bias = jnp.stack([high, middle, decay_bias - high - middle])
    return jnp.concatenate([
        decay_down.T, norm_gain[None], wide(head_gain[None]), wide(bias),
        jnp.zeros((24 - RANK - 5, depth), jnp.bfloat16), wide(decay_up),
    ], axis=0)


def per_device(activations, norm_gain, query_matrix, key_weight, value_weight, decay_down, decay_up,
               decay_bias, head_gain, output_matrix):
    section = lax.axis_index("section")
    core = lax.axis_index("dp") % 2
    tensor = lax.axis_index("tensor")
    y, z = tensor // Z, tensor % Z
    q, k, v, o = query_matrix[0], key_weight[0], value_weight[0], output_matrix[0]

    def half_of(rows):
        return lax.dynamic_slice_in_dim(rows, core * (rows.shape[0] // 2), rows.shape[0] // 2, 0)

    o_half = half_of(o)
    rest = o_half.shape[0] * 5 // 8
    far = {
        "a": jnp.concatenate([half_of(q), half_of(k)], axis=1),
        "b": half_of(v),
        "c": o_half[:rest],
        "d": o_half[rest:],
    }
    far = {n: to_first(value) for n, value in far.items()}
    for n in "abcd":
        far[n + "2"] = to_sibling(far[n])

    mine = activations[:, 0]
    other = yswap(mine)
    pair = jnp.stack([jnp.where(y == 0, mine, other), jnp.where(y == 0, other, mine)], axis=1)
    normed = normalize(pair.astype(jnp.float32), norm_gain[0].astype(jnp.float32)).astype(jnp.bfloat16)
    gathered, down = gather_ring(normed.reshape(4, 16, -1), z, far, {}, decay_down[0])
    pack = make_pack(norm_gain[0], down, decay_up[0], decay_bias[0], head_gain[0])
    far["pack"] = to_first(pack)
    zero = jnp.zeros((), jnp.int32)
    scalars = jnp.stack([z, zero, zero]).astype(jnp.int32)
    scalars = hold(scalars, far, ["a"])
    terms, four_a, four_b = layer_call(scalars, gathered, pack, (q, k, v, o))
    summed = scatter_ring(terms, four_a, four_b, far, {2: ["a2"], 3: ["b"], 4: ["c"]})
    summed = hold(summed.astype(jnp.bfloat16).reshape(2, 2, 16, -1), far, ["b2", "pack"])

    own = jnp.where(section == 0, summed[0], to_second(summed[1]))
    partner = yswap(own)
    stream = jnp.where(section == 0, pair[0], pair[1]).astype(jnp.float32)
    stream = (stream + (own.astype(jnp.float32) + partner.astype(jnp.float32))).astype(jnp.bfloat16)
    pack_second = jnp.where(section == 0, far["pack"], pack)
    normed = normalize(stream.astype(jnp.float32), pack_second[RANK].astype(jnp.float32)).astype(jnp.bfloat16)
    gathered, _ = gather_ring(normed, z, far, {2: ["d"], 3: ["c2"], 4: ["d2"]})
    scalars = jnp.stack([z, 1 - section, core]).astype(jnp.int32)
    terms = layer_call(scalars, gathered, pack_second, (q, k, v, o), [far[n] for n in ("a", "b", "c", "d", "a2", "b2", "c2", "d2")])
    summed = scatter_ring(*terms, far, {})
    keep = jnp.where(y == 0, summed[0], summed[1])
    give = jnp.where(y == 0, summed[1], summed[0]).astype(jnp.bfloat16)
    got = yswap(give)
    base = jnp.where(y == 0, stream[0], stream[1]).astype(jnp.float32)
    return (base + (keep + got.astype(jnp.float32))).astype(jnp.bfloat16)[None, None]


def solution(mesh):
    return jax.shard_map(
        per_device,
        mesh=mesh,
        in_specs=(
            P(None, "dp", "tensor", None),
            P("section", None),
            P("section", None, "tensor"),
            P("section", None, "tensor"),
            P("section", None, "tensor"),
            P("section", None, None),
            P("section", None, "tensor"),
            P("section", "tensor"),
            P("section", "tensor"),
            P("section", "tensor", None),
        ),
        out_specs=P("section", "dp", "tensor", None),
        check_vma=False,
    )
```

```python
import functools

import jax
import jax.numpy as jnp
from jax import lax
from jax.experimental import pallas as pl
from jax.experimental.pallas import tpu as pltpu
from jax.sharding import PartitionSpec as P

Z = 8
KEY = 64
VAL = 128
LEN = 256
RANK = 16
PACK = 40
OFFSETS = (0, 1, 2, 3, 5, 6, 7)


def zp(value):
    return lax.ppermute(value, "tensor", [(y * Z + z, y * Z + (z + 1) % Z) for y in range(2) for z in range(Z)])


def zm(value):
    return lax.ppermute(value, "tensor", [(y * Z + z, y * Z + (z + Z - 1) % Z) for y in range(2) for z in range(Z)])


def yswap(value):
    return lax.ppermute(value, "tensor", [(t, t ^ Z) for t in range(2 * Z)])


def to_second(value):
    n = 2 * Z
    return lax.ppermute(value, ("section", "tensor"), [(t, n + (t ^ Z)) for t in range(n)])


def to_first(value):
    n = 2 * Z
    return lax.ppermute(value, ("section", "tensor"), [(n + t, t ^ Z) for t in range(n)])


def to_sibling(value):
    return lax.ppermute(value, "dp", [(d, d ^ 1) for d in range(lax.axis_size("dp"))])


def normalize(values, gain):
    return values * lax.rsqrt(jnp.mean(values * values, axis=-1, keepdims=True) + 1e-05) * gain


def hold(value, far, names):
    if names:
        value, *arrived = lax.optimization_barrier((value, *[far[n] for n in names]))
        far.update(zip(names, arrived))
    return value


def gather_ring(block, z, far, at, later=0):
    groups, size, depth = block.shape
    half = groups // 2

    def place(x, block, offset, first=0):
        return lax.dynamic_update_slice(x, block, (first, (z + offset) % Z * size, 0))

    p, m = zp(block), zm(block)
    block, p, later = lax.optimization_barrier((block, p, later))
    x = jnp.tile(block, (1, Z, 1))
    for step in (2, 3):
        x = place(place(x, p, Z + 1 - step), m, step - 1)
        p, m = zp(hold(p, far, at.get(step))), zm(m)
    x = place(place(x, p, Z - 3), m, 3)
    p, m = zp(hold(p[:half], far, at.get(4))), zm(m[half:])
    return place(place(x, p, 4), m, 4, half), later


def add(a, b):
    return (a.astype(jnp.float32) + b.astype(jnp.float32)).astype(jnp.bfloat16)


def scatter_ring(terms, four_a, four_b, far, at):
    half = four_a.shape[0]
    p, m = zp(four_a), zm(four_b)
    up = jnp.concatenate([add(terms[3][:half], p), terms[3][half:]], 0)
    down = jnp.concatenate([terms[5][:half], add(terms[5][half:], m)], 0)
    p, m = zp(hold(up, far, at.get(2))), zm(down)
    p, m = zp(hold(add(terms[2], p), far, at.get(3))), zm(add(terms[6], m))
    p, m = zp(hold(add(terms[1], p), far, at.get(4))), zm(add(terms[7], m))
    return terms[0].astype(jnp.float32) + p.astype(jnp.float32) + m.astype(jnp.float32)


def nt(a, b):
    return lax.dot_general(a, b, (((1,), (1,)), ((), ())), preferred_element_type=jnp.float32)


def mix(q, k, v, low, up, bias, gain):
    width = q.shape[1]
    heads = width // KEY
    half = LEN // 2
    bf = jnp.bfloat16
    logits = jnp.dot(low, up, preferred_element_type=jnp.float32) + bias
    log_sig = jnp.minimum(logits, 0.0) - jnp.log(1.0 + jnp.exp(-jnp.abs(logits)))
    decay = jnp.exp(log_sig * (1.0 / 16.0))
    q = q.astype(jnp.float32) * KEY ** -0.5
    row = lax.broadcasted_iota(jnp.int32, (LEN, width), 0)
    lane_head = lax.broadcasted_iota(jnp.int32, (1, width), 1) // KEY
    head_masks = [jnp.where(lane_head == h, 1.0, 0.0).astype(bf) for h in range(heads)]
    i = lax.broadcasted_iota(jnp.int32, (half, half), 0)
    j = lax.broadcasted_iota(jnp.int32, (half, half), 1)
    apart = jnp.where(i > j, i ^ j, 0)
    first, second = slice(0, half), slice(half, LEN)

    def scores(qb, kb):
        lhs = jnp.concatenate([qb * m for m in head_masks], axis=0)
        return nt(lhs, kb).reshape(heads, qb.shape[0], half)

    qb = q.astype(bf)
    att = [jnp.where((i == j)[None], scores(qb[s], k[s]), 0.0) for s in (first, second)]
    q, k, total = q * decay, k.astype(jnp.float32), decay
    for level in range(3):
        b = 1 << level
        qb, kb = q.astype(bf), k.astype(bf)
        mask = ((apart >> level) == 1)[None]
        att = [jnp.where(mask, scores(qb[s], kb[s]), a) for s, a in zip((first, second), att)]
        upper = (row & b) != 0
        other = jnp.where(upper, pltpu.roll(total, b, 0), pltpu.roll(total, LEN - b, 0))
        q = jnp.where(upper, q * other, q)
        k = jnp.where(upper, k, k * other)
        total = total * other
    total = total.reshape(LEN // 8, 8, width)
    for level in range(3, 7):
        b = 1 << level
        pairs = half // (2 * b)
        kb = k.astype(bf)
        q = q.reshape(2 * pairs, 2, b, width)
        qb = q[:, 1].astype(bf).reshape(2, half // 2, width)
        mask = ((apart >> level) == 1).astype(jnp.int32).reshape(pairs, 2, b, half)[:, 1] == 1
        for n, s in enumerate((first, second)):
            a = att[n].reshape(heads, pairs, 2, b, half)
            upper = jnp.where(mask[None], scores(qb[n], kb[s]).reshape(heads, pairs, b, half), a[:, :, 1])
            att[n] = jnp.stack([a[:, :, 0], upper], axis=2).reshape(heads, half, half)
        total = total.reshape(2 * pairs, 2, 1, 8, width)
        begins, ends = total[:, 0], total[:, 1]
        upper = (q[:, 1].reshape(2 * pairs, b // 8, 8, width) * begins).reshape(2 * pairs, b, width)
        q = jnp.stack([q[:, 0], upper], axis=1).reshape(LEN, width)
        k = k.reshape(2 * pairs, 2, b, width)
        lower = (k[:, 0].reshape(2 * pairs, b // 8, 8, width) * ends).reshape(2 * pairs, b, width)
        k = jnp.stack([lower, k[:, 1]], axis=1).reshape(LEN, width)
        total = begins * ends
    across = scores(q[second].astype(bf), k[first].astype(bf))
    outs = []
    for h in range(heads):
        vh = v[:, h * VAL:(h + 1) * VAL]
        top = jnp.dot(att[0][h].astype(bf), vh[first], preferred_element_type=jnp.float32)
        bottom = jnp.dot(jnp.concatenate([across[h], att[1][h]], axis=1).astype(bf), vh,
                         preferred_element_type=jnp.float32)
        mixed = jnp.concatenate([top, bottom], axis=0)
        scale = lax.rsqrt(jnp.maximum(jnp.mean(mixed * mixed, axis=-1, keepdims=True), 1.0))
        outs.append((mixed * scale * gain[:, h * VAL:(h + 1) * VAL]).astype(bf))
    return jnp.concatenate(outs, axis=1)


def layer_kernel(groups, n_halves, scalars, *refs):
    at = 0

    def take(count):
        nonlocal at
        out = refs[at:at + count]
        at += count
        return out

    x, pack, q_src, k_src, v_src, o_src = take(6)
    halves = take(n_halves)
    outs = take(9)
    w, wo, y, gated, sem = take(5)
    half = groups // 2
    z, fetched, core = scalars[0], scalars[1], scalars[2]
    depth = x.shape[1]
    wide = w.shape[2]

    sources = [(q_src, slice(None)), (k_src, slice(None)), (v_src, slice(0, wide)), (v_src, slice(wide, 2 * wide)),
               (o_src, slice(None))]
    targets = [w.at[0], w.at[1], w.at[2], w.at[3], wo]

    def own_copy(index):
        src, columns = sources[index]
        return pltpu.make_async_copy(src.at[:, columns], targets[index], sem.at[index])

    def start_halves(index):
        for (a, b, c, d), side in ((halves[0:4], core), (halves[4:8], 1 - core)):
            rows = pl.ds(pl.multiple_of(side * (depth // 2), depth // 2), depth // 2)
            rest = c.shape[0]
            c_rows = pl.ds(pl.multiple_of(side * wide, wide), rest)
            d_rows = pl.ds(pl.multiple_of(side * wide + rest, 32), wide - rest)
            copies = (
                ((a.at[:, 0:wide], w.at[0, rows, :]),),
                ((a.at[:, wide:2 * wide], w.at[1, rows, :]),),
                ((b.at[:, 0:wide], w.at[2, rows, :]),),
                ((b.at[:, wide:], w.at[3, rows, :]),),
                ((c, wo.at[c_rows, :]), (d, wo.at[d_rows, :])),
            )
            for src, dst in copies[index]:
                pltpu.make_async_copy(src, dst, sem.at[index]).start()

    def start(index):
        if n_halves:
            pl.when(fetched == 0)(own_copy(index).start)
            pl.when(fetched == 1)(functools.partial(start_halves, index))
        else:
            own_copy(index).start()

    start(0)
    start(1)
    low = nt(x[...], pack[0:RANK, :]).astype(jnp.bfloat16)

    for index in range(4):
        own_copy(index).wait()
        if index < 3:
            start(index + 2)
        y[index] = jnp.dot(x[...], w[index], preferred_element_type=jnp.float32).astype(jnp.bfloat16)
    gain = pack[17:18, 0:2 * wide].astype(jnp.float32)
    bias = sum(pack[r:r + 1, 0:wide].astype(jnp.float32) for r in (18, 19, 20))
    up = pack[24:24 + RANK, 0:wide]
    for n in range(groups // 2):
        s = slice(n * LEN, (n + 1) * LEN)
        v = jnp.concatenate([y[2, s, :], y[3, s, :]], axis=1)
        mixed = mix(y[0, s, :], y[1, s, :], v, low[s], up, bias, gain)
        for g in range(2):
            for to in range(Z):
                at = pl.multiple_of((lax.rem(to - z + Z, Z) * groups + 2 * n + g) * 16, 16)
                gated[pl.ds(at, 16), :] = mixed[g * 128 + to * 16:g * 128 + to * 16 + 16]
    own_copy(4).wait()
    step = 512
    for c in range(depth // step):
        cols = slice(c * step, (c + 1) * step)
        part = jnp.dot(gated[...], wo[:, cols], preferred_element_type=jnp.float32).astype(jnp.bfloat16)
        part = part.reshape(Z, groups, 16, step)
        for n, offset in enumerate(OFFSETS):
            outs[n][:, :, cols] = part[offset]
        outs[7][:, :, cols] = part[4, 0:half]
        outs[8][:, :, cols] = part[4, half:groups]


def layer_call(scalars, gathered, pack, weights, halves=()):
    groups, _, depth = gathered.shape
    count = groups * 128
    bf = jnp.bfloat16
    part = jax.ShapeDtypeStruct((groups // 2, 16, depth), bf)
    hbm = pl.BlockSpec(memory_space=pltpu.HBM)
    vmem = pl.BlockSpec(memory_space=pltpu.VMEM)
    wide = weights[0].shape[1]
    operands = [gathered.reshape(count, depth), pack, *weights, *halves]
    outs = pl.pallas_call(
        functools.partial(layer_kernel, groups, len(halves)),
        out_shape=[jax.ShapeDtypeStruct((groups, 16, depth), bf)] * 7 + [part] * 2,
        in_specs=[pl.BlockSpec(memory_space=pltpu.SMEM)] + [vmem] * 2 + [hbm] * (4 + len(halves)),
        out_specs=[vmem] * 9,
        scratch_shapes=[
            pltpu.VMEM((4, depth, wide), bf),
            pltpu.VMEM((2 * wide, depth), bf),
            pltpu.VMEM((4, count, wide), bf),
            pltpu.VMEM((count, 2 * wide), bf),
            pltpu.SemaphoreType.DMA((5,)),
        ],
        compiler_params=pltpu.CompilerParams(vmem_limit_bytes=50 * 1024 * 1024),
        cost_estimate=pl.CostEstimate(flops=count * depth, bytes_accessed=count * depth, transcendentals=0),
    )(scalars, *operands)
    return dict(zip(OFFSETS, outs[:7])), outs[7], outs[8]


def make_pack(norm_gain, decay_down, decay_up, decay_bias, head_gain):
    depth = norm_gain.shape[0]

    def wide(rows):
        return jnp.pad(rows.astype(jnp.bfloat16), ((0, 0), (0, depth - rows.shape[1])))

    high = lax.reduce_precision(decay_bias, 8, 7)
    middle = lax.reduce_precision(decay_bias - high, 8, 7)
    bias = jnp.stack([high, middle, decay_bias - high - middle])
    return jnp.concatenate([
        decay_down.T, norm_gain[None], wide(head_gain[None]), wide(bias),
        jnp.zeros((24 - RANK - 5, depth), jnp.bfloat16), wide(decay_up),
    ], axis=0)


def per_device(activations, norm_gain, query_matrix, key_weight, value_weight, decay_down, decay_up,
               decay_bias, head_gain, output_matrix):
    section = lax.axis_index("section")
    core = lax.axis_index("dp") % 2
    tensor = lax.axis_index("tensor")
    y, z = tensor // Z, tensor % Z
    q, k, v, o = query_matrix[0], key_weight[0], value_weight[0], output_matrix[0]

    def half_of(rows):
        return lax.dynamic_slice_in_dim(rows, core * (rows.shape[0] // 2), rows.shape[0] // 2, 0)

    o_half = half_of(o)
    rest = o_half.shape[0] * 5 // 8
    o_first, o_last = lax.optimization_barrier((o_half[:rest], o_half[rest:]))
    far = {
        "a": jnp.concatenate([half_of(q), half_of(k)], axis=1),
        "b": half_of(v),
        "c": o_first,
        "d": o_last,
    }
    far = {n: to_first(value) for n, value in far.items()}
    for n in "abcd":
        far[n + "2"] = to_sibling(far[n])

    mine = activations[:, 0]
    other = yswap(mine)
    pair = jnp.stack([jnp.where(y == 0, mine, other), jnp.where(y == 0, other, mine)], axis=1)
    normed = normalize(pair.astype(jnp.float32), norm_gain[0].astype(jnp.float32)).astype(jnp.bfloat16)
    small = (decay_down[0], decay_up[0], decay_bias[0], head_gain[0])
    gathered, small = gather_ring(normed.reshape(4, 16, -1), z, far, {}, small)
    pack = make_pack(norm_gain[0], *small)
    far["pack"] = to_first(pack)
    zero = jnp.zeros((), jnp.int32)
    scalars = jnp.stack([z, zero, zero]).astype(jnp.int32)
    scalars = hold(scalars, far, ["a"])
    terms, four_a, four_b = layer_call(scalars, gathered, pack, (q, k, v, o))
    summed = scatter_ring(terms, four_a, four_b, far, {2: ["a2"], 3: ["b"], 4: ["c"]})
    summed = hold(summed.astype(jnp.bfloat16).reshape(2, 2, 16, -1), far, ["b2", "pack"])

    own = jnp.where(section == 0, summed[0], to_second(summed[1]))
    partner = yswap(own)
    stream = jnp.where(section == 0, pair[0], pair[1]).astype(jnp.float32)
    stream = (stream + (own.astype(jnp.float32) + partner.astype(jnp.float32))).astype(jnp.bfloat16)
    pack_second = jnp.where(section == 0, far["pack"], pack)
    normed = normalize(stream.astype(jnp.float32), pack_second[RANK].astype(jnp.float32)).astype(jnp.bfloat16)
    gathered, _ = gather_ring(normed, z, far, {2: ["d"], 3: ["c2"], 4: ["d2"]})
    scalars = jnp.stack([z, 1 - section, core]).astype(jnp.int32)
    terms = layer_call(scalars, gathered, pack_second, (q, k, v, o), [far[n] for n in ("a", "b", "c", "d", "a2", "b2", "c2", "d2")])
    summed = scatter_ring(*terms, far, {})
    keep = jnp.where(y == 0, summed[0], summed[1])
    give = jnp.where(y == 0, summed[1], summed[0]).astype(jnp.bfloat16)
    got = yswap(give)
    base = jnp.where(y == 0, stream[0], stream[1]).astype(jnp.float32)
    return (base + (keep + got.astype(jnp.float32))).astype(jnp.bfloat16)[None, None]


def solution(mesh):
    return jax.shard_map(
        per_device,
        mesh=mesh,
        in_specs=(
            P(None, "dp", "tensor", None),
            P("section", None),
            P("section", None, "tensor"),
            P("section", None, "tensor"),
            P("section", None, "tensor"),
            P("section", None, None),
            P("section", None, "tensor"),
            P("section", "tensor"),
            P("section", "tensor"),
            P("section", "tensor", None),
        ),
        out_specs=P("section", "dp", "tensor", None),
        check_vma=False,
    )
```
